32 devices in a mesh: segment: 2 (over y), dp: 16 (over z, x, core).
Axes of the slice: x: 2, y: 2, z: 4, core: 2. Of those that a mesh axis runs over, the one named last changes fastest.
Arguments:
- patches: bfloat16 [2, 4096, 1024], P('segment', 'dp'), may hold values from -6 to 6
- cotangent: bfloat16 [2, 16384, 512], P('segment', 'dp'), may hold values from -6 to 6
- image_quads: int32 [2, 16, 8], P(None, 'dp'), may hold values from 1 to 128, 256 in all within a row
- keep_pick: int32 [2, 4096], P(None, 'dp'), may hold values from 0 to 3
- image_gsd: float32 [2, 16, 8], P(None, 'dp'), may hold values from 0.5 to 2
- enc_gains: bfloat16 [2, 1024], replicated, may hold values from 0.5 to 1.5
- enc_biases: bfloat16 [6, 1024], replicated, may hold values from -1.796875 to 1.796875
- enc_qkv: bfloat16 [1024, 3072], replicated, may hold values from -0.1875 to 0.1875
- enc_proj: bfloat16 [1024, 1024], replicated, may hold values from -1.5 to 1.5
- enc_fc1: bfloat16 [1024, 4096], replicated, may hold values from -0.1875 to 0.1875
- enc_fc1_bias: bfloat16 [4096], replicated, may hold values from -1.796875 to 1.796875
- enc_fc2: bfloat16 [4096, 1024], replicated, may hold values from -0.09375 to 0.09375
- dec_embed: bfloat16 [1024, 512], replicated, may hold values from -0.1875 to 0.1875
- dec_gains: bfloat16 [2, 512], replicated, may hold values from 0.5 to 1.5
- dec_biases: bfloat16 [8, 512], replicated, may hold values from -1.796875 to 1.796875
- dec_qkv: bfloat16 [512, 1536], replicated, may hold values from -0.25 to 0.25
- dec_proj: bfloat16 [512, 512], replicated, may hold values from -3 to 3
- dec_fc1: bfloat16 [512, 2048], replicated, may hold values from -0.25 to 0.25
- dec_fc1_bias: bfloat16 [2048], replicated, may hold values from -1.796875 to 1.796875
- dec_fc2: bfloat16 [2048, 512], replicated, may hold values from -0.125 to 0.125
Outputs:
- patch_grads: bfloat16 [2, 4096, 1024], P('segment', 'dp')
- grad_enc_gains: float32 [2, 1024], P('segment', 'dp')
- grad_enc_biases: float32 [6, 1024], P('segment', 'dp')
- grad_enc_qkv: float32 [1024, 3072], P('dp', 'segment')
- grad_enc_proj: float32 [1024, 1024], P('dp', 'segment')
- grad_enc_fc1: float32 [1024, 4096], P('dp', 'segment')
- grad_enc_fc1_bias: float32 [4096], P(('segment', 'dp'))
- grad_enc_fc2: float32 [4096, 1024], P('dp', 'segment')
- grad_dec_embed: float32 [1024, 512], P('dp', 'segment')
- grad_dec_gains: float32 [2, 512], P('segment', 'dp')
- grad_dec_biases: float32 [8, 512], P('segment', 'dp')
- grad_dec_qkv: float32 [512, 1536], P('dp', 'segment')
- grad_dec_proj: float32 [512, 512], P('dp', 'segment')
- grad_dec_fc1: float32 [512, 2048], P('dp', 'segment')
- grad_dec_fc1_bias: float32 [2048], P(('segment', 'dp'))
- grad_dec_fc2: float32 [2048, 512], P('dp', 'segment')
The draws below stay inside these ranges and needn't reach their ends.
Inputs may be any that keep to these rules, and one draw needn't show every extreme that they name: `image_quads`: the 8 sizes of each row (one micro-batch, one index of dp) sum to 256; the largest is exactly 128.
All inputs are finite; a program needn't handle non-finite values.
Results may differ from the reference program's by a relative error of at most 0.018.
Values may be sent and summed in bfloat16 or wider, within the bound.
No kernel may reach another device: no remote copies, remote signals or barrier semaphores. Data moves between devices by JAX's collectives and lax.ppermute only.
A program may use at most 448 MiB of HBM per device.

```python
import math
import jax
import jax.numpy as jnp
import numpy as np
from jax import lax

D_ENC = 1024
HEADS = 16
FF_ENC = 4096
D_DEC = 512
FF_DEC = 2048
MICRO = 2
PATCH_MB = 1024
IMGS = 8
QUADS = 256
N_DP = 16


def with_ends(result, rng, least, high):
    longest = result.shape.index(max(result.shape))
    spots = []
    for shift in (0, 1):
        where = [jax.random.randint(jax.random.fold_in(rng, axis), (), 0, length) for axis, length in enumerate(result.shape)]
        where[longest] = (where[longest] + shift) % result.shape[longest]
        spots.append(tuple(where))
    return result.at[spots[0]].set(least).at[spots[1]].set(high)


def level_of(own_key, shape, pieces, least, high):
    def one(dim, parts):
        steps = jax.random.uniform(jax.random.fold_in(jax.random.fold_in(own_key, 6), dim), (parts,), jnp.float32, least / len(pieces), high / len(pieces))
        return jnp.repeat(jnp.exp(steps), shape[dim] // parts).reshape((-1,) + (1,) * (len(shape) - dim - 1))

    level = one(*pieces[0])
    for cut in pieces[1:]:
        level = level * one(*cut)
    return level


def profile(amount, total, limit, skew):
    loads = [(1 << 20) // math.isqrt(standing ** skew) + 1 for standing in range(2, amount + 1)]
    rest, given = total - limit - (amount - 1), [1] * (amount - 1)
    while rest > 0:
        free = [i for i in range(amount - 1) if given[i] < limit]
        mass, left = sum([loads[i] for i in free]), rest
        for i in free:
            more = min(limit - given[i], max(1, left * loads[i] // mass), rest)
            given[i] = given[i] + more
            rest = rest - more
    return np.array([limit] + given)


def ragged(rng, count, total, reach, lean):
    if count == 2:
        one = jax.random.randint(rng, (), max(1, total - reach), min(reach, total - 1) + 1)
        return jnp.stack([one, total - one])
    sizes = jnp.asarray(profile(count, total, reach, lean), jnp.int32)
    couples = (count - 1) // 2
    source_of, taker = sizes[1:1 + 2 * couples:2], sizes[2:2 + 2 * couples:2]
    room = jnp.minimum(source_of - 1, reach - taker)
    moved = jax.random.randint(jax.random.fold_in(rng, 1), (couples,), 0, 1 << 20) % (room + 1)
    sizes = sizes.at[1:1 + 2 * couples:2].set(source_of - moved).at[2:2 + 2 * couples:2].set(taker + moved)
    return sizes[jax.random.permutation(jax.random.fold_in(rng, 2), count)]


def scatter_about(key, shape, scale, most, cuts=(), kind=jnp.bfloat16):
    level = level_of(key, shape, cuts, -0.22, 0.18) if cuts else 1.0
    result = jax.random.normal(key, shape, jnp.float32) * scale * level
    return jnp.minimum(jnp.maximum(result, -most), most).astype(kind)


def setup_inputs(seed: int = 0) -> dict:
    seeds = jax.random.split(jax.random.key(seed), 21)
    patches = scatter_about(seeds[0], (MICRO, N_DP * QUADS, D_ENC), 1.0, 6.0, ((0, 2), (1, 16)))
    cotangent = scatter_about(seeds[1], (MICRO, N_DP * PATCH_MB, D_DEC), 1.0, 6.0, ((0, 2), (1, 16)))
    image_quads = jax.vmap(lambda own: ragged(own, IMGS, QUADS, QUADS // 2, 2))(jax.random.split(seeds[2], MICRO * N_DP)).reshape((MICRO, N_DP, IMGS)).astype(jnp.int32)
    keep_pick = with_ends(jax.random.randint(seeds[3], (MICRO, N_DP * QUADS), 0, 4), jax.random.fold_in(seeds[3], 1), 0, 3).astype(jnp.int32)
    image_gsd = jnp.clip(jnp.exp(math.log(2.0) - 1.3862944 * jax.random.uniform(seeds[4], (MICRO, N_DP, IMGS), jnp.float32) ** level_of(seeds[4], (MICRO, N_DP, IMGS), ((1, 16),), -0.2, 0.2)), 0.5, 2.0)
    enc_gains = jnp.clip(1.0 + 0.1 * jax.random.normal(seeds[5], (2, D_ENC), jnp.float32), 0.5, 1.5).astype(jnp.bfloat16)
    enc_biases = scatter_about(seeds[6], (6, D_ENC), 0.3, 1.796875)
    enc_qkv = scatter_about(seeds[7], (D_ENC, 3 * D_ENC), D_ENC ** -0.5, 0.1875)
    enc_proj = scatter_about(seeds[8], (D_ENC, D_ENC), (max(D_ENC // 64, 1)) ** -0.5, 1.5)
    enc_fc1 = scatter_about(seeds[9], (D_ENC, FF_ENC), D_ENC ** -0.5, 0.1875)
    enc_fc1_bias = scatter_about(seeds[10], (FF_ENC,), 0.3, 1.796875)
    enc_fc2 = scatter_about(seeds[11], (FF_ENC, D_ENC), FF_ENC ** -0.5, 0.09375)
    dec_embed = scatter_about(seeds[12], (D_ENC, D_DEC), D_ENC ** -0.5, 0.1875)
    dec_gains = jnp.clip(1.0 + 0.1 * jax.random.normal(seeds[13], (2, D_DEC), jnp.float32), 0.5, 1.5).astype(jnp.bfloat16)
    dec_biases = scatter_about(seeds[14], (8, D_DEC), 0.3, 1.796875)
    dec_qkv = scatter_about(seeds[15], (D_DEC, 3 * D_DEC), D_DEC ** -0.5, 0.25)
    dec_proj = scatter_about(seeds[16], (D_DEC, D_DEC), (max(D_DEC // 128, 1)) ** -0.5, 3.0)
    dec_fc1 = scatter_about(seeds[17], (D_DEC, FF_DEC), D_DEC ** -0.5, 0.25)
    dec_fc1_bias = scatter_about(seeds[18], (FF_DEC,), 0.3, 1.796875)
    dec_fc2 = scatter_about(seeds[19], (FF_DEC, D_DEC), FF_DEC ** -0.5, 0.125)
    return {"patches": patches, "cotangent": cotangent, "image_quads": image_quads, "keep_pick": keep_pick, "image_gsd": image_gsd, "enc_gains": enc_gains, "enc_biases": enc_biases, "enc_qkv": enc_qkv, "enc_proj": enc_proj, "enc_fc1": enc_fc1, "enc_fc1_bias": enc_fc1_bias, "enc_fc2": enc_fc2, "dec_embed": dec_embed, "dec_gains": dec_gains, "dec_biases": dec_biases, "dec_qkv": dec_qkv, "dec_proj": dec_proj, "dec_fc1": dec_fc1, "dec_fc1_bias": dec_fc1_bias, "dec_fc2": dec_fc2}


@jax.custom_vjp
def low(v):
    return lax.optimization_barrier(v.astype(jnp.bfloat16)).astype(jnp.float32)

@jax.custom_vjp
def low_back(v):
    return v

def low_keep(v):
    return (low(v), None)

def low_pass(kept, grad):
    return (grad,)

def back_keep(v):
    return (v, None)

def back_low(kept, grad):
    return (low(grad),)
low.defvjp(low_keep, low_pass)
low_back.defvjp(back_keep, back_low)
EPSILON = 1e-06
MASKED = -1e+30

def matmul(left_side, right_side):
    return jnp.dot(left_side, right_side, precision=lax.Precision.HIGHEST)

def layer_norm(values, gain, shift):
    centred = values - lax.optimization_barrier(jnp.mean(values, -1, keepdims=True))
    spread = lax.optimization_barrier(jnp.mean(centred * centred, -1, keepdims=True))
    return centred * lax.rsqrt(spread + EPSILON) * gain + shift

def gelu_exact(values):
    return 0.5 * values * (1.0 + jax.scipy.special.erf(values * 0.7071067811865476))

def layout(quad_sizes, pick_row, gsd_row, feature_width):
    quad_total = pick_row.shape[0]
    quad_ends = jnp.cumsum(quad_sizes).astype(jnp.int32)
    quad_index = jnp.arange(quad_total, dtype=jnp.int32)
    passed = quad_index[:, None] >= quad_ends[None, :]
    image_of = lax.optimization_barrier(jnp.sum(passed.astype(jnp.int32), 1)).astype(jnp.int32)
    first_quad = lax.optimization_barrier(jnp.sum(jnp.where(passed, quad_sizes[None, :], 0), 1)).astype(jnp.int32)
    owned_by = image_of[:, None] == jnp.arange(quad_sizes.shape[0], dtype=jnp.int32)[None, :]
    gsd_quad = lax.optimization_barrier(jnp.sum(jnp.where(owned_by, gsd_row[None, :], 0.0), 1))
    slot_index = jnp.arange(4 * quad_total, dtype=jnp.int32)
    slot_image = jnp.repeat(image_of, 4)
    visible = slot_index % 4 == jnp.repeat(pick_row, 4)
    offsets = (slot_index - 4 * jnp.repeat(first_quad, 4)).astype(gsd_row.dtype)
    angles = offsets * jnp.repeat(gsd_quad, 4)
    frequency = jnp.exp(jnp.arange(feature_width // 2).astype(gsd_row.dtype) * (-2.0 * math.log(10000.0) / feature_width))
    phases = angles[:, None] * frequency[None, :]
    pos_code = jnp.concatenate([jnp.sin(phases), jnp.cos(phases)], 1)
    same_quad = image_of[:, None] == image_of[None, :]
    same_slot = slot_image[:, None] == slot_image[None, :]
    return (same_quad, same_slot, visible, pos_code)

def attention(packed, same_image):
    row_count = packed.shape[0]
    feature_width = packed.shape[1] // 3
    head_size = feature_width // HEADS
    split_rows = packed.reshape(row_count, 3, HEADS, head_size).transpose(1, 2, 0, 3)

    def one_head(head_parts):
        query_head, key_head, value_head = head_parts
        scores = low_back(matmul(query_head, key_head.T) * head_size ** (-0.5))
        scores = jnp.where(same_image, scores, MASKED)
        largest = lax.optimization_barrier(jnp.max(scores, -1, keepdims=True))
        weights = jnp.exp(scores - largest)
        probability = weights / lax.optimization_barrier(jnp.sum(weights, -1, keepdims=True))
        return matmul(low(probability), value_head)
    heads_out = lax.map(jax.checkpoint(one_head), (split_rows[0], split_rows[1], split_rows[2]))
    return heads_out.transpose(1, 0, 2).reshape(row_count, feature_width)

def block(values, params, same_image):
    gain_rows, biases, w_qkv, w_out, w_up, up_bias, w_down = params
    normed = low(layer_norm(values, gain_rows[0], biases[0]))
    qkv_bias = jnp.concatenate([biases[1], jnp.zeros_like(biases[1]), biases[2]])
    packed = low(low_back(matmul(normed, w_qkv) + qkv_bias))
    mixed_heads = low(low_back(attention(packed, same_image)))
    residual = values + low_back(matmul(mixed_heads, w_out) + biases[3])
    normed_two = low(layer_norm(residual, gain_rows[1], biases[4]))
    hidden = low(gelu_exact(low_back(matmul(normed_two, w_up) + up_bias)))
    return residual + low_back(matmul(hidden, w_down) + biases[5])

def reference(patches, cotangent, image_quads, keep_pick, image_gsd, enc_gains, enc_biases, enc_qkv, enc_proj, enc_fc1, enc_fc1_bias, enc_fc2, dec_embed, dec_gains, dec_biases, dec_qkv, dec_proj, dec_fc1, dec_fc1_bias, dec_fc2):
    row_count = MICRO * N_DP
    patch_rows = patches.astype(jnp.float32).reshape(row_count, QUADS, D_ENC)
    target_rows = cotangent.astype(jnp.float32).reshape(row_count, PATCH_MB, D_DEC)
    quad_rows = image_quads.reshape(row_count, IMGS)
    pick_rows = keep_pick.reshape(row_count, QUADS)
    gsd_rows = image_gsd.reshape(row_count, IMGS)
    enc_params = tuple((weight.astype(jnp.float32) for weight in (enc_gains, enc_biases, enc_qkv, enc_proj, enc_fc1, enc_fc1_bias, enc_fc2)))
    dec_params = tuple((weight.astype(jnp.float32) for weight in (dec_gains, dec_biases, dec_qkv, dec_proj, dec_fc1, dec_fc1_bias, dec_fc2, dec_embed)))

    def one_row(patch_row, quad_sizes, pick_row, gsd_row, enc_set, dec_set):
        same_quad, same_slot, visible, pos_code = layout(quad_sizes, pick_row, gsd_row, D_DEC)
        enc_out = low(low_back(block(patch_row, enc_set, same_quad)))
        embedded = low_back(matmul(enc_out, dec_set[7]) + dec_set[1][6])
        spread_rows = jnp.repeat(embedded, 4, axis=0)
        tokens = jnp.where(visible[:, None], spread_rows, dec_set[1][7][None, :]) + pos_code
        return block(tokens, dec_set[:7], same_slot)

    def forward(patch_all, enc_set, dec_set):
        checked = jax.checkpoint(one_row)

        def scan_step(carry_on, row_data):
            return (carry_on, checked(row_data[0], row_data[1], row_data[2], row_data[3], enc_set, dec_set))
        unused, row_outputs = lax.scan(scan_step, 0, (patch_all, quad_rows, pick_rows, gsd_rows))
        return row_outputs
    unused, pullback = jax.vjp(forward, patch_rows, enc_params, dec_params)
    grad_patches, grad_enc, grad_dec = pullback(target_rows)
    patch_grads = grad_patches.reshape(MICRO, N_DP * QUADS, D_ENC).astype(jnp.bfloat16)
    return (patch_grads, grad_enc[0], grad_enc[1], grad_enc[2], grad_enc[3], grad_enc[4], grad_enc[5], grad_enc[6], grad_dec[7], grad_dec[0], grad_dec[1], grad_dec[2], grad_dec[3], grad_dec[4], grad_dec[5], grad_dec[6])
```

```python
import functools
import math

import jax
import jax.numpy as jnp
import numpy as np
from jax import lax
from jax.experimental import pallas as pl
from jax.experimental.pallas import tpu as pltpu
from jax.sharding import PartitionSpec as P

BF, F32, I32 = jnp.bfloat16, jnp.float32, jnp.int32
HEADS = 16
EPSILON = 1e-06
LOG2E = 1.4426950408889634
LN2 = 0.6931471805599453
FAR = -1e30
TABLE = 96
VMEM_LIMIT = 60 * 1024 * 1024
SOME = pl.CostEstimate(flops=4000000000, bytes_accessed=10**6, transcendentals=0)
MORE = pl.CostEstimate(flops=8 * 10**9, bytes_accessed=10**6, transcendentals=0)
WAIT = pl.CostEstimate(flops=12 * 10**9, bytes_accessed=10**6, transcendentals=0)
REST = pl.CostEstimate(flops=12 * 10**9, bytes_accessed=10**6, transcendentals=0)
LONGER = pl.CostEstimate(flops=2 * 10**11, bytes_accessed=10**8, transcendentals=0)
LONG = pl.CostEstimate(flops=3 * 10**10, bytes_accessed=10**8, transcendentals=0)
TINY = pl.CostEstimate(flops=1000, bytes_accessed=1000, transcendentals=0)
ANY = pl.BlockSpec(memory_space=pl.ANY)
VM = pl.BlockSpec(memory_space=pltpu.VMEM)
SM = pl.BlockSpec(memory_space=pltpu.SMEM)


def dot(a, b, ca, cb):
    return lax.dot_general(a, b, (((ca,), (cb,)), ((), ())), preferred_element_type=F32)


def norm_parts(v):
    c = v - jnp.mean(v, -1, keepdims=True)
    r = lax.rsqrt(jnp.mean(c * c, -1, keepdims=True) + EPSILON)
    return c * r, r


def norm_back(v, gain, e):
    n, r = norm_parts(v)
    eg = e * gain
    dv = r * (eg - jnp.mean(eg, -1, keepdims=True) - n * jnp.mean(eg * n, -1, keepdims=True))
    return dv, jnp.sum(e * n, 0, keepdims=True), jnp.sum(e, 0, keepdims=True)


def gelu_parts(u):
    size = jnp.abs(u)
    t = 1.0 / (1.0 + 0.2316419 * size)
    bell = jnp.exp2(u * u * (-0.5 * LOG2E))
    poly = 1.330274429 * t - 1.821255978
    poly = poly * t + 1.781477937
    poly = poly * t - 0.356563782
    poly = poly * t + 0.319381530
    dens = bell * 0.3989422804014327
    tail = poly * t * dens
    cdf = jnp.where(u >= 0.0, 1.0 - tail, tail)
    return u * cdf, cdf + u * dens


def three(v):
    hi = v.astype(BF)
    rest = v - hi.astype(F32)
    mid = rest.astype(BF)
    low = (rest - mid.astype(F32)).astype(BF)
    return hi.astype(F32), mid.astype(F32), low.astype(F32)


def stack16(rows, width):
    at = lax.broadcasted_iota(I32, (16, width), 0)
    out = jnp.zeros((16, width), F32)
    for i, row in rows:
        out = jnp.where(at == i, row, out)
    return out


def image_codes(quads, sizes_ref, m, images):
    end = 0
    img = jnp.zeros(quads.shape, I32)
    first = jnp.zeros(quads.shape, I32)
    for k in range(images):
        end = end + sizes_ref[m, 0, k]
        over = quads >= end
        img = img + over.astype(I32)
        first = jnp.where(over, end, first)
    return img, first


def mask_rows(img, images, width):
    at = lax.broadcasted_iota(I32, (16, width), 0)
    same = at == img
    inside = at < images
    q_rows = jnp.where(inside & same, 1.0, 0.0)
    k_rows = jnp.where(inside & jnp.logical_not(same), FAR, 0.0)
    k_rows = jnp.where((at >= images) & (at < images + 3), 1.0, k_rows)
    return q_rows, k_rows


def attend_forward(packed, mixed, lse, q_rows, k_rows, h, width, dh, cols, images):
    q = packed[pl.ds(pl.multiple_of(h * dh, dh), dh), cols]
    k = packed[pl.ds(pl.multiple_of(width + h * dh, dh), dh), cols]
    v = packed[pl.ds(pl.multiple_of(2 * width + h * dh, dh), dh), cols]
    qa = jnp.concatenate([q, q_rows[:, cols]], 0)
    ka = jnp.concatenate([k, k_rows[:, cols]], 0)
    s = dot(ka, qa, 0, 0)
    top = jnp.max(s, 0, keepdims=True)
    e = jnp.exp2(s - top).astype(BF)
    va = jnp.concatenate([v, jnp.ones((16, v.shape[1]), BF)], 0)
    o = dot(va, e, 1, 0)
    total = o[dh : dh + 1]
    mixed[pl.ds(pl.multiple_of(h * dh, dh), dh), cols] = (o[:dh] / total).astype(BF)
    lse[pl.ds(h, 1), cols] = top + jnp.log2(total)


def attend_backward(
    packed, mixed, lse, d_mixed, d_packed, q_rows, k_rows, h, width, dh, cols, images
):
    rows = [pl.ds(pl.multiple_of(part * width + h * dh, dh), dh) for part in range(3)]
    q, k, v = (packed[r, cols] for r in rows)
    count = q.shape[1]
    neg = three(-lse[pl.ds(h, 1), cols])
    extra = stack16([(images + i, neg[i]) for i in range(3)], count)
    qa = jnp.concatenate([q, (q_rows[:, cols].astype(F32) + extra).astype(BF)], 0)
    ka = jnp.concatenate([k, k_rows[:, cols]], 0)
    p = jnp.exp2(dot(ka, qa, 0, 0))
    do = d_mixed[rows[0], cols]
    centre = jnp.sum(do.astype(F32) * mixed[rows[0], cols].astype(F32), 0, keepdims=True)
    neg = three(-centre)
    da = jnp.concatenate([do, stack16([(i, neg[i]) for i in range(3)], count).astype(BF)], 0)
    at = lax.broadcasted_iota(I32, (16, count), 0)
    va = jnp.concatenate([v, jnp.where(at < 3, 1.0, 0.0).astype(BF)], 0)
    ds = (p * dot(va, da, 0, 0)).astype(BF)
    dv = dot(do, p.astype(BF), 1, 1)
    dk = dot(q, ds, 1, 1) * LN2
    dq = dot(k, ds, 1, 0) * (dh**-0.5)
    d_packed[rows[0], cols] = dq.astype(BF)
    d_packed[rows[1], cols] = dk.astype(BF)
    d_packed[rows[2], cols] = dv.astype(BF)


def attend_forward_kept(packed, mixed, scale, kept, q_rows, k_rows, h, side, width, dh, cols):
    q = packed[pl.ds(pl.multiple_of(h * dh, dh), dh), cols]
    k = packed[pl.ds(pl.multiple_of(width + h * dh, dh), dh), cols]
    v = packed[pl.ds(pl.multiple_of(2 * width + h * dh, dh), dh), cols]
    qa = jnp.concatenate([q, q_rows[:, cols]], 0)
    ka = jnp.concatenate([k, k_rows[:, cols]], 0)
    s = dot(ka, qa, 0, 0)
    top = jnp.max(s, 0, keepdims=True)
    e = jnp.exp2(s - top).astype(BF)
    kept[2 * h + side] = e
    va = jnp.concatenate([v, jnp.ones((16, v.shape[1]), BF)], 0)
    o = dot(va, e, 1, 0)
    part = 1.0 / o[dh : dh + 1]
    mixed[pl.ds(pl.multiple_of(h * dh, dh), dh), cols] = (o[:dh] * part).astype(BF)
    scale[pl.ds(h, 1), cols] = part


def attend_backward_kept(packed, mixed, scale, kept, d_mixed, h, width, dh, sides):
    rows = [pl.ds(pl.multiple_of(part * width + h * dh, dh), dh) for part in range(3)]
    read = [[packed[r, cols] for r in rows] for cols in sides]
    grads = []
    for side, cols in enumerate(sides):
        q, k, v = read[side]
        count = q.shape[1]
        part = scale[pl.ds(h, 1), cols]
        do = d_mixed[rows[0], cols].astype(F32) * part
        centre = jnp.sum(do * mixed[rows[0], cols].astype(F32), 0, keepdims=True)
        do = do.astype(BF)
        neg = three(-centre)
        da = jnp.concatenate([do, stack16([(i, neg[i]) for i in range(3)], count).astype(BF)], 0)
        at = lax.broadcasted_iota(I32, (16, count), 0)
        va = jnp.concatenate([v, jnp.where(at < 3, 1.0, 0.0).astype(BF)], 0)
        e = kept[2 * h + side]
        ds = (e.astype(F32) * dot(va, da, 0, 0)).astype(BF)
        dv = dot(e, do.T, 1, 0).T
        dk = dot(ds, q.T, 1, 0).T * LN2
        dq = dot(k, ds, 1, 0) * (dh**-0.5)
        grads.append((dq, dk, dv))
    for cols, parts in zip(sides, grads):
        for r, part in zip(rows, parts):
            packed[r, cols] = part.astype(BF)


def enc_forward_kernel(
    info, sizes, x_ref, gains, biases, up_bias, wqkv_h, wo_h, w1_h, w2_h,
    out_ref, xs_h, xk_h, hs_h, hk_h, packed_h, lse, mixed_h, resid_h, slope_h,
    wqkv, wo, w1, w2, packed, mixed, resid, slope, xt, ht, n2_s, acc, qr, kr, sems,
):
    m, c, x = info[0], info[1], info[2]
    images = sizes.shape[2]
    tokens, width = x_ref.shape
    hidden = w1.shape[1]
    dh = width // HEADS
    nzx = xt.shape[1]
    r_d = width // (2 * nzx)
    r_h = hidden // (2 * nzx)
    tile = 512
    copies = [pltpu.make_async_copy(wqkv_h, wqkv, sems.at[0])]
    copies.append(pltpu.make_async_copy(wo_h, wo, sems.at[1]))
    copies.append(pltpu.make_async_copy(w1_h, w1, sems.at[2]))
    copies.append(pltpu.make_async_copy(w2_h, w2, sems.at[3]))
    for copy in copies:
        copy.start()
    gain = gains[...].astype(F32)
    bias = biases[...].astype(F32)

    def keep_rows(values, start):
        for a in range(nzx):
            for cc in range(2):
                at = (a * 2 + cc) * r_d
                xt[cc, a, start : start + r_d, :] = values[at : at + r_d]

    quads = lax.broadcasted_iota(I32, (1, tokens), 1)
    img, _ = image_codes(quads, sizes, m, images)
    q_rows, k_rows = mask_rows(img, images, tokens)
    qr[...] = q_rows.astype(BF)
    kr[...] = k_rows.astype(BF)
    n, _ = norm_parts(x_ref[...].astype(F32))
    n1 = (n * gain[0:1] + bias[0:1]).astype(BF)
    keep_rows(n1.T, 0)
    copies[0].wait()
    for part in range(3):
        cols = slice(part * width, (part + 1) * width)
        got = dot(n1, wqkv[:, cols], 1, 0)
        if part == 0:
            got = (got + bias[1:2]) * (dh**-0.5 * LOG2E)
        if part == 2:
            got = got + bias[2:3]
        packed[cols, :] = got.astype(BF).T

    def head(h, carry):
        attend_forward(packed, mixed, lse, qr, kr, h, width, dh, slice(0, tokens), images)
        return carry

    lax.fori_loop(0, HEADS, head, 0, unroll=2)
    outs = [pltpu.make_async_copy(packed, packed_h, sems.at[4])]
    outs.append(pltpu.make_async_copy(mixed, mixed_h, sems.at[5]))
    for copy in outs:
        copy.start()
    mix = mixed[...]
    keep_rows(mix, r_d)
    copies[1].wait()
    res = x_ref[...].astype(F32) + dot(mix, wo[...], 0, 0) + bias[3:4]
    resid[...] = res
    n, _ = norm_parts(res)
    n2 = (n * gain[1:2] + bias[4:5]).astype(BF)
    n2_s[...] = n2
    keep_rows(n2.T, 2 * r_d)
    more = [
        pltpu.make_async_copy(resid, resid_h, sems.at[6]),
        pltpu.make_async_copy(xt.at[1 - c], xs_h, sems.at[7]),
        pltpu.make_async_copy(xt.at[c], xk_h, sems.at[8]),
    ]
    for copy in more:
        copy.start()
    outs = outs + more
    acc[...] = res + bias[5:6]
    copies[2].wait()
    copies[3].wait()
    per = tile // (2 * r_h)

    def ffn(t, carry):
        cols = pl.ds(pl.multiple_of(t * tile, tile), tile)
        u = dot(n2_s[...], w1[:, cols], 1, 0) + up_bias[:, cols].astype(F32)
        hid, dif = gelu_parts(u)
        hid = hid.astype(BF)
        slope[:, cols] = dif.astype(BF)
        hid_t = hid.T
        for a in range(per):
            for cc in range(2):
                at = (a * 2 + cc) * r_h
                zx = t * per + a
                ht[zx & 1, zx >> 1, cc, :, :] = hid_t[at : at + r_h]
        acc[...] += dot(hid, w2[cols, :], 1, 0)
        return carry

    lax.fori_loop(0, hidden // tile, ffn, 0)
    out_ref[...] = acc[...].astype(BF)
    more = [
        pltpu.make_async_copy(ht.at[1 - x], hs_h, sems.at[2]),
        pltpu.make_async_copy(ht.at[x], hk_h, sems.at[3]),
        pltpu.make_async_copy(slope, slope_h, sems.at[9]),
    ]
    for copy in more:
        copy.start()
    for copy in outs + more:
        copy.wait()


def enc_forward(info, sizes, x, gains, biases, up_bias, wqkv, wo, w1, w2, nzx):
    tokens, width = x.shape
    hidden = w1.shape[1]
    rows = 3 * width // (2 * nzx)
    half = jax.ShapeDtypeStruct((nzx, rows, tokens), BF)
    h_shape = (nzx // 2, 2, hidden // (2 * nzx), tokens)
    h_half = jax.ShapeDtypeStruct(h_shape, BF)
    return pl.pallas_call(
        enc_forward_kernel,
        out_shape=(
            jax.ShapeDtypeStruct((tokens, width), BF),
            half,
            half,
            h_half,
            h_half,
            jax.ShapeDtypeStruct((3 * width, tokens), BF),
            jax.ShapeDtypeStruct((HEADS, tokens), F32),
            jax.ShapeDtypeStruct((width, tokens), BF),
            jax.ShapeDtypeStruct((tokens, width), F32),
            jax.ShapeDtypeStruct((tokens, hidden), BF),
        ),
        in_specs=[SM, SM, VM, VM, VM, VM, ANY, ANY, ANY, ANY],
        out_specs=(VM, ANY, ANY, ANY, ANY, ANY, VM, ANY, ANY, ANY),
        scratch_shapes=[
            pltpu.VMEM(wqkv.shape, BF),
            pltpu.VMEM(wo.shape, BF),
            pltpu.VMEM(w1.shape, BF),
            pltpu.VMEM(w2.shape, BF),
            pltpu.VMEM((3 * width, tokens), BF),
            pltpu.VMEM((width, tokens), BF),
            pltpu.VMEM((tokens, width), F32),
            pltpu.VMEM((tokens, hidden), BF),
            pltpu.VMEM((2, nzx, rows, tokens), BF),
            pltpu.VMEM((2,) + h_shape, BF),
            pltpu.VMEM((tokens, width), BF),
            pltpu.VMEM((tokens, width), F32),
            pltpu.VMEM((16, tokens), BF),
            pltpu.VMEM((16, tokens), BF),
            pltpu.SemaphoreType.DMA((10,)),
        ],
        compiler_params=pltpu.CompilerParams(vmem_limit_bytes=VMEM_LIMIT),
        cost_estimate=TINY,
        name="enc_forward",
    )(info, sizes, x, gains, biases, up_bias, wqkv, wo, w1, w2)


def enc_ffn_back_kernel(
    dy_ref, resid, slope, gains, w1_h, w2_h, *rest
):
    du_ref, dres, small, w1, w2, acc, sems = rest[-7:]
    tokens, width = dy_ref.shape
    hidden = w1.shape[1]
    tile = 512
    parts = hidden // tile
    loads = []
    for t in range(parts):
        at = pl.ds(t * tile, tile)
        loads.append(pltpu.make_async_copy(w2_h.at[at, :], w2.at[at, :], sems.at[2 * t]))
        loads.append(pltpu.make_async_copy(w1_h.at[:, at], w1.at[:, at], sems.at[2 * t + 1]))
    for copy in loads:
        copy.start()
    gain = gains[...].astype(F32)
    dy = dy_ref[...]
    total = jnp.zeros((tokens, width), F32)
    acc[...] = total
    small[...] = jnp.zeros(small.shape, F32)
    for t in range(parts):
        loads[2 * t].wait()
        loads[2 * t + 1].wait()
        cols = slice(t * tile, (t + 1) * tile)
        dh = dot(dy, w2[cols, :], 1, 1)
        du = (dh * slope[:, cols].astype(F32)).astype(BF)
        du_ref[:, cols] = du
        sums = jnp.sum(du.astype(F32), 0, keepdims=True)
        row, col = divmod(t * tile, width)
        small[8 + row : 9 + row, col : col + tile] = sums
        acc[...] += dot(du, w1[:, cols], 1, 1)
    dv, d_gain, d_shift = norm_back(resid[...], gain[1:2], acc[...])
    dyf = dy.astype(F32)
    res = dyf + dv
    dres[...] = res
    da = res.astype(BF)
    du_ref[:, hidden:] = da
    small[1:2, :] = d_gain
    small[5:6, :] = jnp.sum(da.astype(F32), 0, keepdims=True)
    small[6:7, :] = d_shift
    small[7:8, :] = jnp.sum(dyf, 0, keepdims=True)


def enc_ffn_back(dy, resid, slope, gains, w1, w2, deps):
    tokens, width = dy.shape
    hidden = w1.shape[1]
    return pl.pallas_call(
        enc_ffn_back_kernel,
        out_shape=(
            jax.ShapeDtypeStruct((tokens, hidden + width), BF),
            jax.ShapeDtypeStruct((tokens, width), F32),
            jax.ShapeDtypeStruct((16, width), F32),
        ),
        in_specs=[VM, VM, VM, VM] + [ANY] * (2 + len(deps)),
        out_specs=(VM, VM, VM),
        scratch_shapes=[
            pltpu.VMEM(w1.shape, BF),
            pltpu.VMEM(w2.shape, BF),
            pltpu.VMEM((tokens, width), F32),
            pltpu.SemaphoreType.DMA((2 * (hidden // 512),)),
        ],
        compiler_params=pltpu.CompilerParams(vmem_limit_bytes=VMEM_LIMIT),
        cost_estimate=LONGER,
        name="enc_ffn_back",
    )(dy, resid, slope, gains, w1, w2, *deps)


def enc_att_back_kernel(
    info, sizes, x_ref, da_h, dres, packed, lse, mixed, gains, small_a, small_d, wqkv_h, wo_h, *rest
):
    dx_ref, d_two, d_one, wqkv, wo, da, d_mixed, d_packed, qr, kr, sems = rest[-11:]
    m = info[0]
    images = sizes.shape[2]
    tokens, width = x_ref.shape
    dh = width // HEADS
    loads = [
        pltpu.make_async_copy(wo_h, wo, sems.at[0]),
        pltpu.make_async_copy(wqkv_h, wqkv, sems.at[1]),
        pltpu.make_async_copy(da_h.at[:, pl.ds(da_h.shape[1] - width, width)], da, sems.at[2]),
    ]
    for copy in loads:
        copy.start()
    gain = gains[...].astype(F32)
    quads = lax.broadcasted_iota(I32, (1, tokens), 1)
    img, _ = image_codes(quads, sizes, m, images)
    q_rows, k_rows = mask_rows(img, images, tokens)
    qr[...] = q_rows.astype(BF)
    kr[...] = k_rows.astype(BF)
    loads[0].wait()
    loads[2].wait()
    d_mixed[...] = dot(wo[...], da[...], 1, 1).astype(BF)

    def head(h, carry):
        attend_backward(
            packed, mixed, lse, d_mixed, d_packed, qr, kr, h, width, dh, slice(0, tokens), images
        )
        return carry

    lax.fori_loop(0, HEADS, head, 0, unroll=2)
    loads[1].wait()
    dp = d_packed[...]
    part = width // 2
    for half in range(2):
        for j in range(2):
            at, to = (half * 3 + j) * part, (half * 2 + j) * part
            d_two[to : to + part, :] = dp[at : at + part]
        at = (half * 3 + 2) * part
        d_one[half * part : (half + 1) * part, :] = dp[at : at + part]
    table = d_one.shape[0] - TABLE
    d_one[width:table, :] = jnp.zeros((table - width, tokens), BF)
    e = dot(wqkv[...], dp, 1, 0).T
    dv, d_gain, d_shift = norm_back(x_ref[...].astype(F32), gain[0:1], e)
    dx_ref[...] = (dres[...] + dv).astype(BF)
    ones = jnp.ones((16, tokens), BF)
    sums = dot(ones, dp, 1, 1)
    mine = {0: d_gain, 2: d_shift, 3: sums[0:1, :width], 4: sums[0:1, 2 * width :]}
    rows = [mine[i] if i in mine else small_a[i : i + 1, :] for i in range(16)]
    rows = jnp.concatenate(rows, 0).astype(BF)
    piece = tokens
    for p in range(width // piece):
        at = table + p * 16
        d_one[at : at + 16, :] = rows[:, p * piece : (p + 1) * piece]
    rows = small_d[...].astype(BF)
    for p in range(rows.shape[1] // piece):
        at = table + (width // piece + p) * 16
        d_one[at : at + 16, :] = rows[:, p * piece : (p + 1) * piece]


def enc_att_back(
    info, sizes, x, da, dres, packed, lse, mixed, gains, small_a, small_d, wqkv, wo, deps
):
    tokens, width = x.shape
    return pl.pallas_call(
        enc_att_back_kernel,
        out_shape=(
            jax.ShapeDtypeStruct((tokens, width), BF),
            jax.ShapeDtypeStruct((2 * width, tokens), BF),
            jax.ShapeDtypeStruct(((width // TABLE + 2) * TABLE, tokens), BF),
        ),
        in_specs=[SM, SM, VM, ANY] + [VM] * 7 + [ANY] * (2 + len(deps)),
        out_specs=(VM, VM, VM),
        scratch_shapes=[
            pltpu.VMEM(wqkv.shape, BF),
            pltpu.VMEM(wo.shape, BF),
            pltpu.VMEM((tokens, width), BF),
            pltpu.VMEM((width, tokens), BF),
            pltpu.VMEM((3 * width, tokens), BF),
            pltpu.VMEM((16, tokens), BF),
            pltpu.VMEM((16, tokens), BF),
            pltpu.SemaphoreType.DMA((3,)),
        ],
        compiler_params=pltpu.CompilerParams(vmem_limit_bytes=VMEM_LIMIT),
        cost_estimate=TINY,
        name="enc_att_back",
    )(info, sizes, x, da, dres, packed, lse, mixed, gains, small_a, small_d, wqkv, wo, *deps)


def wave_codes(phases):
    turn = jnp.floor(phases * 0.6366197723675814 + 0.5)
    r = phases - turn * 1.5703125
    r = r - turn * 4.837512969970703125e-4
    r = r - turn * 7.54978995489188216e-8
    sq = r * r
    sn = -1.9515295891e-4 * sq + 8.3321608736e-3
    sn = (sn * sq - 1.6666654611e-1) * sq * r + r
    cs = 2.443315711809948e-5 * sq - 1.388731625493765e-3
    cs = (cs * sq + 4.166664568298827e-2) * sq * sq - 0.5 * sq + 1.0
    quarter = turn.astype(I32) & 3
    odd = (quarter & 1) == 1
    sine = jnp.where(odd, cs, sn)
    cosine = jnp.where(odd, sn, cs)
    sine = jnp.where(quarter >= 2, -sine, sine)
    cosine = jnp.where((quarter == 1) | (quarter == 2), -cosine, cosine)
    return sine, cosine


def decoder_kernel(
    info, sizes, gsd, pick_ref, freq, act_ref, cot_ref, gains, biases, up_bias,
    wemb, wqkv, wo_h, w1_h, w2_h,
    dact_ref, dh_own, dh_other, gs_h, gk_h, small,
    x_s, n_s, packed, mixed, scale, res_s, n2_s, hid_s, du_s, cot_s, dmix, kept, emb_s, demb_s,
    grads, wo, w1, w2, qr, kr, sems,
):
    m, c = info[0], info[1]
    loads = [
        pltpu.make_async_copy(wo_h, wo, sems.at[4]),
        pltpu.make_async_copy(w1_h, w1, sems.at[5]),
        pltpu.make_async_copy(w2_h, w2, sems.at[6]),
    ]
    for copy in loads:
        copy.start()
    images = sizes.shape[2]
    quads, e_width = act_ref.shape
    slots, width = cot_ref.shape
    hidden = w1.shape[1]
    dh = width // HEADS
    chunk = 512
    parts = slots // chunk
    nzx = grads.shape[1]
    half = width // 2
    gain = gains[...].astype(F32)
    bias = biases[...].astype(F32)

    start, best, seen = 0, 0, 0
    for k in range(images):
        size = sizes[m, 0, k]
        start = jnp.where(size > best, seen, start)
        best = jnp.maximum(size, best)
        seen = seen + size

    lane = lax.broadcasted_iota(I32, (1, slots), 1)
    img, _ = image_codes(((lane + 4 * start) & (slots - 1)) >> 2, sizes, m, images)
    q_rows, k_rows = mask_rows(img, images, slots)
    qr[...] = q_rows.astype(BF)
    kr[...] = k_rows.astype(BF)
    emb = dot(act_ref[...], wemb[...], 1, 0) + bias[6:7]
    hi = emb.astype(BF)
    emb_s[0] = hi
    emb_s[1] = (emb - hi.astype(F32)).astype(BF)
    picks = pick_ref[pl.ds(m, 1), :]

    def slot_of(i, count):
        row = lax.broadcasted_iota(I32, (chunk, count), 0) + i * chunk
        return (row + 4 * start) & (slots - 1)

    def shown(i):
        slot = slot_of(i, quads)
        col = lax.broadcasted_iota(I32, (chunk, quads), 1)
        return (col == (slot >> 2)) & (picks == (slot & 3))

    def enter(i, carry):
        rows = pl.ds(pl.multiple_of(i * chunk, chunk), chunk)
        hit = shown(i)
        one = jnp.where(hit, 1.0, 0.0)
        one_b = one.astype(BF)
        vis = jnp.sum(one, 1, keepdims=True)
        slot = slot_of(i, 1)
        quad = slot >> 2
        end = 0
        first = jnp.zeros((chunk, 1), I32)
        ratio = jnp.full((chunk, 1), gsd[m, 0, 0])
        for k in range(images - 1):
            end = end + sizes[m, 0, k]
            over = quad >= end
            first = jnp.where(over, end, first)
            ratio = jnp.where(over, gsd[m, 0, k + 1], ratio)
        angle = (slot - 4 * first).astype(F32) * ratio
        sine, cosine = wave_codes(angle * freq[...])
        tok = dot(one_b, emb_s[0], 1, 0) + dot(one_b, emb_s[1], 1, 0) + (1.0 - vis) * bias[7:8]
        x_s[rows, :half] = tok[:, :half] + sine
        x_s[rows, half:] = tok[:, half:] + cosine
        n, _ = norm_parts(x_s[rows, :])
        n1 = (n * gain[0:1] + bias[0:1]).astype(BF)
        n_s[rows, :] = n1
        for part in range(3):
            cols = slice(part * width, (part + 1) * width)
            got = dot(n1, wqkv[:, cols], 1, 0)
            if part == 0:
                got = (got + bias[1:2]) * (dh**-0.5 * LOG2E)
            if part == 2:
                got = got + bias[2:3]
            packed[cols, rows] = got.astype(BF).T
        move = lax.broadcasted_iota(I32, (chunk, slots), 1) == slot_of(i, slots)
        cot_s[rows, :] = dot(jnp.where(move, 1.0, 0.0).astype(BF), cot_ref[...], 1, 0).astype(BF)
        return carry

    lax.fori_loop(0, parts, enter, 0)
    sides = [slice(0, slots // 2), slice(slots // 2, slots)]

    def head(h, carry):
        for side, cols in enumerate(sides):
            attend_forward_kept(
                packed, mixed, scale, kept, qr, kr, h, side, width, dh, cols
            )
        return carry

    lax.fori_loop(0, HEADS, head, 0)
    for copy in loads:
        copy.wait()
    small[...] = jnp.zeros(small.shape, F32)
    tile = 512

    def middle(i, carry):
        rows = pl.ds(pl.multiple_of(i * chunk, chunk), chunk)
        res = x_s[rows, :] + dot(mixed[:, rows], wo[...], 0, 0) + bias[3:4]
        n, _ = norm_parts(res)
        n2 = (n * gain[1:2] + bias[4:5]).astype(BF)
        n2_s[rows, :] = n2
        dy = cot_s[rows, :]
        acc = jnp.zeros((chunk, width), F32)
        for t in range(hidden // tile):
            cols = slice(t * tile, (t + 1) * tile)
            u = dot(n2, w1[:, cols], 1, 0) + up_bias[:, cols].astype(F32)
            hid, dif = gelu_parts(u)
            hid_s[rows, cols] = hid.astype(BF)
            du = (dot(dy, w2[cols, :], 1, 1) * dif).astype(BF)
            du_s[rows, cols] = du
            row, col = divmod(t * tile, width)
            small[10 + row : 11 + row, col : col + tile] += jnp.sum(
                du.astype(F32), 0, keepdims=True
            )
            acc = acc + dot(du, w1[:, cols], 1, 1)
        dv, d_gain, d_shift = norm_back(res, gain[1:2], acc)
        dyf = dy.astype(F32)
        dres = dyf + dv
        res_s[rows, :] = dres
        da = dres.astype(BF)
        small[1:2, :] += d_gain
        small[5:6, :] += jnp.sum(da.astype(F32), 0, keepdims=True)
        small[6:7, :] += d_shift
        small[7:8, :] += jnp.sum(dyf, 0, keepdims=True)
        dmix[:, rows] = dot(wo[...], da, 1, 1).astype(BF)
        return carry

    lax.fori_loop(0, parts, middle, 0)

    def place(values, offset, r, wide):
        for a in range(values.shape[0] // (2 * r)):
            for cc in range(2):
                at = (a * 2 + cc) * r
                for y in range(2):
                    for j in range(wide):
                        lo = (y * wide + j) * half
                        grads[cc, a, y, offset + j * r : offset + (j + 1) * r, :] = values[
                            at : at + r, lo : lo + half
                        ]

    r_e, r_d, r_h = e_width // (2 * nzx), width // (2 * nzx), hidden // (2 * nzx)
    at_emb, at_qkv = 0, r_e
    at_out = at_qkv + 3 * r_d
    at_up = at_out + r_d
    at_down = at_up + (hidden // width) * r_d
    cot_all = cot_s[...]
    for t in range(hidden // 256):
        got = dot(hid_s[:, t * 256 : (t + 1) * 256], cot_all, 0, 0).astype(BF)
        for a in range(256 // r_h):
            blk = t * (256 // r_h) + a
            for y in range(2):
                grads[blk % 2, blk // 2, y, at_down : at_down + r_h, :] = got[
                    a * r_h : (a + 1) * r_h, y * half : (y + 1) * half
                ]
    n2_t = n2_s[...].T
    wide = hidden // width
    for t in range(hidden // half):
        got = dot(n2_t, du_s[:, t * half : (t + 1) * half], 1, 0).astype(BF)
        y, j = divmod(t, wide)
        for blk in range(2 * nzx):
            lo = at_up + j * r_d
            grads[blk % 2, blk // 2, y, lo : lo + r_d, :] = got[blk * r_d : (blk + 1) * r_d]
    place(dot(mixed[...], res_s[...].astype(BF), 1, 0).astype(BF), at_out, r_d, 1)

    def head_back(h, carry):
        attend_backward_kept(packed, mixed, scale, kept, dmix, h, width, dh, sides)
        return carry

    late = at_out if r_d % 16 == 0 else 0
    early = pl.ds(late, grads.shape[3] - late)
    outs = [
        pltpu.make_async_copy(grads.at[1 - c, :, :, early], gs_h.at[:, :, early], sems.at[0]),
        pltpu.make_async_copy(grads.at[c, :, :, early], gk_h.at[:, :, early], sems.at[1]),
    ]
    if late:
        for copy in outs:
            copy.start()
    lax.fori_loop(0, HEADS, head_back, 0)
    n1_t = n_s[...].T
    for t in range(3 * width // half):
        got = dot(n1_t, packed[t * half : (t + 1) * half, :], 1, 1).astype(BF)
        y, j = divmod(t, 3)
        for blk in range(2 * nzx):
            lo = at_qkv + j * r_d
            grads[blk % 2, blk // 2, y, lo : lo + r_d, :] = got[blk * r_d : (blk + 1) * r_d]
    sums = dot(jnp.ones((16, slots), BF), packed[...], 1, 1)
    small[3:4, :] = sums[0:1, :width]
    small[4:5, :] = sums[0:1, 2 * width :]
    demb_s[...] = jnp.zeros(demb_s.shape, F32)

    def leave(i, carry):
        rows = pl.ds(pl.multiple_of(i * chunk, chunk), chunk)
        e = dot(wqkv[...], packed[:, rows], 1, 0).T
        dv, d_gain, d_shift = norm_back(x_s[rows, :], gain[0:1], e)
        dx = res_s[rows, :] + dv
        hit = jnp.where(shown(i), 1.0, 0.0)
        vis = jnp.sum(hit, 1, keepdims=True)
        demb_s[...] += dot(hit.astype(BF), dx.astype(BF), 0, 0)
        small[0:1, :] += d_gain
        small[2:3, :] += d_shift
        small[9:10, :] += jnp.sum((1.0 - vis) * dx, 0, keepdims=True)
        return carry

    lax.fori_loop(0, parts, leave, 0)
    demb = demb_s[...]
    small[8:9, :] = jnp.sum(demb, 0, keepdims=True)
    demb = demb.astype(BF)
    dact = dot(demb, wemb[...], 1, 1)
    dact_ref[...] = dact.astype(BF)
    lower, upper = dact[:, : e_width // 2], dact[:, e_width // 2 :]
    dh_own[...] = jnp.where(m == 0, lower, upper).astype(BF)
    dh_other[...] = jnp.where(m == 0, upper, lower).astype(BF)
    place(dot(act_ref[...], demb, 0, 0).astype(BF), at_emb, r_e, 1)
    if late:
        first = pl.ds(0, late)
        rest = [
            pltpu.make_async_copy(grads.at[1 - c, :, :, first], gs_h.at[:, :, first], sems.at[2]),
            pltpu.make_async_copy(grads.at[c, :, :, first], gk_h.at[:, :, first], sems.at[3]),
        ]
        for copy in rest:
            copy.start()
        outs = outs + rest
    else:
        for copy in outs:
            copy.start()
    for copy in outs:
        copy.wait()


def decoder(info, sizes, gsd, picks, act, cot, gains, biases, up_bias, wemb, wqkv, wo, w1, w2, nzx):
    quads, e_width = act.shape
    slots, width = cot.shape
    hidden = w1.shape[1]
    total = e_width + 4 * width + hidden
    rows = (total + hidden // width * width) // (2 * nzx)
    freq = np.exp(np.arange(width // 2) * (-2.0 * math.log(10000.0) / width))
    freq = jnp.asarray(freq.astype(np.float32)[None, :])
    block = jax.ShapeDtypeStruct((nzx, 2, rows, width // 2), BF)
    return pl.pallas_call(
        decoder_kernel,
        out_shape=(
            jax.ShapeDtypeStruct((quads, e_width), BF),
            jax.ShapeDtypeStruct((quads, e_width // 2), BF),
            jax.ShapeDtypeStruct((quads, e_width // 2), BF),
            block,
            block,
            jax.ShapeDtypeStruct((16, width), F32),
        ),
        in_specs=[SM, SM, SM] + [VM] * 9 + [ANY] * 3,
        out_specs=(VM, VM, VM, ANY, ANY, VM),
        scratch_shapes=[
            pltpu.VMEM((slots, width), F32),
            pltpu.VMEM((slots, width), BF),
            pltpu.VMEM((3 * width, slots), BF),
            pltpu.VMEM((width, slots), BF),
            pltpu.VMEM((HEADS, slots), F32),
            pltpu.VMEM((slots, width), F32),
            pltpu.VMEM((slots, width), BF),
            pltpu.VMEM((slots, hidden), BF),
            pltpu.VMEM((slots, hidden), BF),
            pltpu.VMEM((slots, width), BF),
            pltpu.VMEM((width, slots), BF),
            pltpu.VMEM((2 * HEADS, slots // 2, slots // 2), BF),
            pltpu.VMEM((2, quads, width), BF),
            pltpu.VMEM((quads, width), F32),
            pltpu.VMEM((2, nzx, 2, rows, width // 2), BF),
            pltpu.VMEM(wo.shape, BF),
            pltpu.VMEM(w1.shape, BF),
            pltpu.VMEM(w2.shape, BF),
            pltpu.VMEM((16, slots), BF),
            pltpu.VMEM((16, slots), BF),
            pltpu.SemaphoreType.DMA((8,)),
        ],
        compiler_params=pltpu.CompilerParams(vmem_limit_bytes=VMEM_LIMIT),
        cost_estimate=TINY,
        name="decoder",
    )(info, sizes, gsd, picks, freq, act, cot, gains, biases, up_bias, wemb, wqkv, wo, w1, w2)


def pick_call(body, sel, arrays, specs, out_shape, out_specs, grid, name, deps=(), scratch=(), cost=None):
    count = len(arrays)

    def run(*refs):
        body(refs[0], *refs[1 : 1 + count], *refs[1 + count + len(deps) :])

    return pl.pallas_call(
        run,
        grid_spec=pltpu.PrefetchScalarGridSpec(
            num_scalar_prefetch=1,
            grid=grid,
            in_specs=list(specs) + [ANY] * len(deps),
            out_specs=out_specs,
            scratch_shapes=list(scratch),
        ),
        out_shape=out_shape,
        compiler_params=pltpu.CompilerParams(vmem_limit_bytes=VMEM_LIMIT),
        cost_estimate=cost or TINY,
        name=name,
    )(sel, *arrays, *deps)


def down_grad(sel, hids, dys, deps):
    nz, _, r, tokens = hids[0].shape
    half = dys[0].shape[1]
    count = len(hids)

    def body(s, *refs):
        got = dot(refs[0][...], refs[count][...], 1, 0)
        for i in range(1, count):
            got = got + dot(refs[i][...], refs[count + i][...], 1, 0)
        refs[-1][...] = got.astype(BF)

    lhs = pl.BlockSpec((None, None, r, tokens), lambda z, s: (z, s[0], 0, 0))
    rhs = pl.BlockSpec((tokens, half), lambda z, s: (0, 0))
    return pick_call(
        body, sel, tuple(hids) + tuple(dys), [lhs] * count + [rhs] * count,
        jax.ShapeDtypeStruct((nz, r, half), BF),
        pl.BlockSpec((None, r, half), lambda z, s: (z, 0, 0)),
        (nz,), "down_grad", deps, (), LONG,
    )


def down_fold(place, hids, dys, got, deps):
    nz, _, r, tokens = hids[0].shape
    half = dys[0].shape[1]
    count = len(hids)

    def body(s, *refs):
        total = dot(refs[0][...], refs[count][...], 1, 0)
        for i in range(1, count):
            total = total + dot(refs[i][...], refs[count + i][...], 1, 0)
        total = (total + refs[2 * count][...].astype(F32)).astype(BF)
        step = pl.program_id(0)

        @pl.when(step < 2)
        def first():
            refs[-2][...] = total

        @pl.when(step >= 2)
        def second():
            refs[-1][...] = total

    def block(i, s):
        base = jnp.where(i < 2, s[2] ^ 1, s[2])
        return jnp.where((i & 1) == 1, 3 - base, base)

    lhs = pl.BlockSpec((None, None, r, tokens), lambda i, s: (block(i, s), s[3] & 1, 0, 0))
    rhs = pl.BlockSpec((tokens, half), lambda i, s: (0, 0))
    more = pl.BlockSpec((None, r, half), lambda i, s: (block(i, s), 0, 0))
    shape = jax.ShapeDtypeStruct((2, r, half), BF)
    outs = (
        pl.BlockSpec((None, r, half), lambda i, s: (jnp.minimum(i, 1), 0, 0)),
        pl.BlockSpec((None, r, half), lambda i, s: (jnp.maximum(i - 2, 0), 0, 0)),
    )
    return pick_call(
        body, place, tuple(hids) + tuple(dys) + (got,), [lhs] * count + [rhs] * count + [more],
        (shape, shape), outs, (4,), "down_fold", deps,
    )


def up_grad(sel, xk, xr, duk, dur, deps):
    nzx, rows, tokens = xk.shape
    r, half = rows // 3, 512
    cols = 4

    def body(s, a, b, da, db, out):
        lhs = a[...].reshape(nzx * r, tokens)
        lhr = b[...].reshape(nzx * r, tokens)
        got = dot(lhs, da[...], 1, 0) + dot(lhr, db[...], 1, 0)
        out[...] = got.astype(BF).reshape(nzx, r, half)

    lhs = pl.BlockSpec((nzx, r, tokens), lambda j, s: (0, 2, 0))
    rhs = pl.BlockSpec((tokens, half), lambda j, s: (0, s[0] * cols + j))
    return pick_call(
        body, sel, (xk, xr, duk, dur), [lhs, lhs, rhs, rhs],
        jax.ShapeDtypeStruct((nzx, cols * r, half), BF),
        pl.BlockSpec((nzx, r, half), lambda j, s: (0, j, 0)),
        (cols,), "up_grad", deps,
    )


def up_turn(place, xk, xr, duk, dur, got, deps):
    nzx, rows, tokens = xk.shape
    nz, r, half, cols = nzx // 2, rows // 3, 512, 4

    def body(s, ag, bg, ak, bk, da, db, gg, gk, give, keep):
        for a, b, g, out in ((ag, bg, gg, give), (ak, bk, gk, keep)):
            total = dot(a[...].reshape(nz * r, tokens), da[...], 1, 0)
            total = total + dot(b[...].reshape(nz * r, tokens), db[...], 1, 0)
            total = total + g[...].reshape(nz * r, half).astype(F32)
            out[...] = total.astype(BF).reshape(nz, r, half)

    def lhs(flip):
        return pl.BlockSpec((nz, None, r, tokens), lambda j, s: (0, s[0] ^ flip, 2, 0))

    def more(flip):
        return pl.BlockSpec((nz, None, r, half), lambda j, s: (0, s[0] ^ flip, j, 0))

    rhs = pl.BlockSpec((tokens, half), lambda j, s: (0, s[1] * cols + j))
    four = (nz, 2, rows, tokens)
    a, b = xk.reshape(four), xr.reshape(four)
    got = got.reshape(nz, 2, cols * r, half)
    shape = jax.ShapeDtypeStruct((nz, cols * r, half), BF)
    out = pl.BlockSpec((nz, r, half), lambda j, s: (0, j, 0))
    return pick_call(
        body, place, (a, b, a, b, duk, dur, got, got),
        [lhs(1), lhs(1), lhs(0), lhs(0), rhs, rhs, more(1), more(0)],
        (shape, shape), (out, out),
        (cols,), "up_turn", deps,
    )


def qk_turn(place, xk, xr, dpk, dpr, got, deps):
    nzx, rows, tokens = xk.shape
    nz, r, half = nzx // 2, rows // 3, 512

    def body(s, a, b, dg, eg, dk, ek, gg, gk, give, keep):
        lhs, lhr = a[...].reshape(nz * r, tokens), b[...].reshape(nz * r, tokens)
        for d, e, g, out in ((dg, eg, gg, give), (dk, ek, gk, keep)):
            total = dot(lhs, d[...], 1, 1) + dot(lhr, e[...], 1, 1)
            total = total + g[...].reshape(nz * r, half).astype(F32)
            out[...] = total.astype(BF).reshape(nz, r, half)

    lhs = pl.BlockSpec((nz, None, r, tokens), lambda j, s: (0, s[0], 0, 0))

    def rhs(flip):
        return pl.BlockSpec((half, tokens), lambda j, s: ((s[1] ^ flip) * 2 + j, 0))

    def more(flip):
        return pl.BlockSpec((nz, None, r, half), lambda j, s: (0, s[1] ^ flip, j, 0))

    four = (nz, 2, rows, tokens)
    shape = jax.ShapeDtypeStruct((nz, 2 * r, half), BF)
    out = pl.BlockSpec((nz, r, half), lambda j, s: (0, j, 0))
    return pick_call(
        body, place, (xk.reshape(four), xr.reshape(four), dpk, dpr, dpk, dpr, got, got),
        [lhs, lhs, rhs(1), rhs(1), rhs(0), rhs(0), more(1), more(0)],
        (shape, shape), (out, out), (2,), "qk_turn", deps,
    )


def table_blocks(r):
    return -(-(TABLE // 2) // r)


def put_table(out, first, table, r):
    lines = table.shape[0]
    for k in range(table_blocks(r)):
        count = min(r, lines - k * r)
        out[first + k, :count] = table[k * r : k * r + count]
        if count < r:
            out[first + k, count:r] = jnp.zeros((r - count, table.shape[1]), BF)


def take_table(ref, first, r):
    lines = TABLE // 2
    parts = [ref[first + k, : min(r, lines - k * r)] for k in range(table_blocks(r))]
    return jnp.concatenate(parts, 0) if len(parts) > 1 else parts[0]


def vo_turn(place, xk, xr, dpk, dpr, dak, dar, got, table, deps):
    nzx, rows, tokens = xk.shape
    nz, r, half = nzx // 2, rows // 3, 512
    tail = table_blocks(r)

    def body(s, ag, bg, ak, bk, d, e, f, h, g, own, give, keep, sums):
        came = g[:nzx].reshape(nz, 2, r, half)
        lower, upper = came[:, 0].astype(F32), came[:, 1].astype(F32)
        first = s[0] == 0
        sides = (jnp.where(first, upper, lower), jnp.where(first, lower, upper))

        def run(dx, ex, cb):
            for a, b, c, out in ((ag, bg, sides[0], give), (ak, bk, sides[1], keep)):
                total = dot(a[...].reshape(nz * r, tokens), dx[...], 1, cb)
                total = total + dot(b[...].reshape(nz * r, tokens), ex[...], 1, cb)
                total = total.reshape(nz, r, half) + c
                out[:nz] = total.astype(BF)

        @pl.when(pl.program_id(0) == 0)
        def qkv():
            run(d, e, 1)
            total = own[...].astype(F32) + take_table(g, nzx, r).astype(F32)
            sums[...] = total.astype(BF)
            put_table(give, nz, total.astype(BF), r)

        @pl.when(pl.program_id(0) == 1)
        def proj():
            run(f, h, 0)
            give[nz:] = jnp.zeros((tail, r, half), BF)

    def lhs(flip):
        return pl.BlockSpec((nz, None, r, tokens), lambda i, s: (0, s[0] ^ flip, i, 0))

    rhs = pl.BlockSpec((half, tokens), lambda i, s: (s[1], 0))
    other = pl.BlockSpec((tokens, half), lambda i, s: (0, dak.shape[1] // half - 2 + s[1]))
    tab = pl.BlockSpec(table.shape, lambda i, s: (0, 0))
    four = (nz, 2, rows, tokens)
    a, b = xk.reshape(four), xr.reshape(four)
    block = lambda n: pl.BlockSpec((n, r, half), lambda i, s: (0, i, 0))
    shape = lambda n: jax.ShapeDtypeStruct((n, 2 * r, half), BF)
    return pick_call(
        body, place, (a, b, a, b, dpk, dpr, dak, dar, got, table),
        [lhs(1), lhs(1), lhs(0), lhs(0), rhs, rhs, other, other, block(nzx + tail), tab],
        (shape(nz + tail), shape(nz), jax.ShapeDtypeStruct(table.shape, BF)),
        (block(nz + tail), block(nz), tab), (2,), "vo_turn", deps,
    )


def qk_grad(sel, xk, xr, dpk, dpr, deps):
    nzx, rows, tokens = xk.shape
    nz, r, half = nzx // 2, rows // 3, 512

    def body(s, a, b, da, db, out):
        lhs = a[...].reshape(nz * r, tokens)
        lhr = b[...].reshape(nz * r, tokens)
        got = dot(lhs, da[...], 1, 1) + dot(lhr, db[...], 1, 1)
        out[...] = got.astype(BF).reshape(nz, 1, r, half)

    lhs = pl.BlockSpec((nz, 1, r, tokens), lambda y, j, s: (0, s[0], 0, 0))
    rhs = pl.BlockSpec((half, tokens), lambda y, j, s: (y * 2 + j, 0))
    split = (nz, 2, rows, tokens)
    return pick_call(
        body, sel, (xk.reshape(split), xr.reshape(split), dpk, dpr), [lhs, lhs, rhs, rhs],
        jax.ShapeDtypeStruct((nz, 2, 2 * r, half), BF),
        pl.BlockSpec((nz, 1, r, half), lambda y, j, s: (0, y, j, 0)),
        (2, 2), "qk_grad", deps,
    )


def vo_grad(sel, xk, xr, dpk, dpr, dak, dar, deps):
    nzx, rows, tokens = xk.shape
    r, half = rows // 3, 512
    top, tail = dpk.shape[0] // TABLE - 1, table_blocks(r)

    def body(s, a, b, da, db, ea, eb, ta, tb, out, table):
        lhs = a[...].reshape(nzx * r, tokens)
        lhr = b[...].reshape(nzx * r, tokens)

        @pl.when(pl.program_id(0) == 0)
        def first():
            got = dot(lhs, da[...], 1, 1) + dot(lhr, db[...], 1, 1)
            out[:nzx] = got.astype(BF).reshape(nzx, r, half)
            total = (ta[...].astype(F32) + tb[...].astype(F32)).astype(BF)
            table[:, :tokens] = total[: TABLE // 2]
            table[:, tokens:] = total[TABLE // 2 :]
            put_table(out, nzx, table[...], r)

        @pl.when(pl.program_id(0) == 1)
        def second():
            got = dot(lhs, ea[...], 1, 0) + dot(lhr, eb[...], 1, 0)
            out[:nzx] = got.astype(BF).reshape(nzx, r, half)
            out[nzx:] = jnp.zeros((tail, r, half), BF)

    lhs = pl.BlockSpec((nzx, r, tokens), lambda i, s: (0, i, 0))
    rhs = pl.BlockSpec((half, tokens), lambda i, s: (s[0], 0))
    other = pl.BlockSpec((tokens, half), lambda i, s: (0, dak.shape[1] // half - 2 + s[0]))
    behind = pl.BlockSpec((TABLE, tokens), lambda i, s: (top, 0))
    shape = (
        jax.ShapeDtypeStruct((nzx + tail, 2 * r, half), BF),
        jax.ShapeDtypeStruct((TABLE // 2, 2 * tokens), BF),
    )
    out = (
        pl.BlockSpec((nzx + tail, r, half), lambda i, s: (0, i, 0)),
        pl.BlockSpec((TABLE // 2, 2 * tokens), lambda i, s: (0, 0)),
    )
    return pick_call(
        body, sel, (xk, xr, dpk, dpr, dak, dar, dpk, dpr),
        [lhs, lhs, rhs, rhs, other, other, behind, behind], shape, out, (2,), "vo_grad", deps,
    )


def to_core(value):
    return lax.ppermute(value, "dp", [(d, d ^ 1) for d in range(lax.axis_size("dp"))])


def to_x(value):
    return lax.ppermute(value, "dp", [(d, d ^ 2) for d in range(lax.axis_size("dp"))])


def to_y(value):
    return lax.ppermute(value, "segment", [(0, 1), (1, 0)])


def to_corner(value):
    count = lax.axis_size("dp")
    pairs = [(s * count + d, (1 - s) * count + (d ^ 2)) for s in range(2) for d in range(count)]
    return lax.ppermute(value, ("segment", "dp"), pairs)


def to_z(value, step):
    count = lax.axis_size("dp")
    return lax.ppermute(value, "dp", [(d, (d + 4 * step) % count) for d in range(count)])


def to_z_pair(value):
    return lax.ppermute(value, "dp", [(d, d ^ 4) for d in range(lax.axis_size("dp"))])


def to_z_mirror(value):
    return lax.ppermute(value, "dp", [(d, d ^ 12) for d in range(lax.axis_size("dp"))])


def summed(refs):
    total = refs[0][...].astype(F32)
    for ref in refs[1:]:
        total = total + ref[...].astype(F32)
    return total


def turn(place, items, extra, deps, cost=None):
    nz = items[0][0].shape[0]
    count = 4 * len(items)

    def body(s, *refs):
        outs = refs[count + len(extra) :]
        for i in range(count // 2):
            outs[i][...] = summed(refs[2 * i : 2 * i + 2]).astype(BF)
        if extra:
            outs[-1][...] = summed(refs[count : count + 2]).astype(BF)

    def spec(shape, which, flip):
        return pl.BlockSpec((None, None) + shape[2:], lambda z, s: (z, s[which] ^ flip, 0, 0))

    arrays, specs, outs, shapes = (), [], [], []
    for kept, got, which in items:
        for flip in (1, 0):
            arrays += (kept, got)
            specs += [spec(kept.shape, which, flip)] * 2
            outs.append(pl.BlockSpec((None,) + kept.shape[2:], lambda z, s: (z, 0, 0)))
            shapes.append(jax.ShapeDtypeStruct((nz,) + kept.shape[2:], BF))
    for table in extra:
        arrays += (table,)
        specs.append(pl.BlockSpec(table.shape, lambda z, s: (0, 0)))
    if extra:
        outs.append(specs[-1])
        shapes.append(jax.ShapeDtypeStruct(extra[0].shape, BF))
    return pick_call(
        body, place, arrays, specs, tuple(shapes), tuple(outs), (nz,), "turn", deps, (), cost
    )


def fold(place, pairs, extra, deps, cost):
    nz, _, half = pairs[0][0].shape
    arrays = tuple(v for pair in pairs for v in pair) + tuple(extra)
    rows = sum(kept.shape[1] for kept, got in pairs) + (extra[0].shape[0] if extra else 0)

    def body(s, *refs):
        give, keep = refs[-2:]
        z = s[2]
        for out, first in ((give, z ^ 1), (keep, z)):
            for i, block in ((0, first), (1, 3 - first)):
                at = 0
                for p in range(len(pairs)):
                    a, b = refs[2 * p], refs[2 * p + 1]
                    r = a.shape[1]
                    out[i, at : at + r] = (a[block].astype(F32) + b[block].astype(F32)).astype(BF)
                    at += r
                if extra:
                    came = take_table(refs[2 * len(pairs) - 1], nz, refs[1].shape[1] // 2)
                    out[i, at:] = (refs[2 * len(pairs)][...].astype(F32) + came.astype(F32)).astype(BF)

    whole = lambda array: pl.BlockSpec(array.shape, lambda i, s: (0,) * array.ndim)
    shape = jax.ShapeDtypeStruct((2, rows, half), BF)
    out = pl.BlockSpec((2, rows, half), lambda i, s: (0, 0, 0))
    return pick_call(
        body, place, arrays, [whole(a) for a in arrays], (shape, shape), (out, out),
        (1,), "fold", deps, (), cost,
    )


def fold_wide(place, kept, got, deps):
    _, rows, cols = kept.shape

    def body(s, a, b, give, keep):
        total = (a[...].astype(F32) + b[...].astype(F32)).astype(BF)
        step = pl.program_id(0)

        @pl.when(step < 2)
        def first():
            give[...] = total

        @pl.when(step >= 2)
        def second():
            keep[...] = total

    def block(i, s):
        base = jnp.where(i < 2, s[2] ^ 1, s[2])
        return jnp.where((i & 1) == 1, 3 - base, base)

    spec = pl.BlockSpec((None, rows, cols), lambda i, s: (block(i, s), 0, 0))
    shape = jax.ShapeDtypeStruct((2, rows, cols), BF)
    outs = (
        pl.BlockSpec((None, rows, cols), lambda i, s: (jnp.minimum(i, 1), 0, 0)),
        pl.BlockSpec((None, rows, cols), lambda i, s: (jnp.maximum(i - 2, 0), 0, 0)),
    )
    return pick_call(
        body, place, (kept, got), [spec, spec], (shape, shape), outs, (4,), "fold_wide", deps
    )


def settle(place, parts, which, deps, cost=None):
    rows, cols = parts[0].shape[-2] // 2, parts[0].shape[-1]
    count = len(parts)

    def body(s, *refs):
        refs[-2][...] = summed(refs[:count]).astype(BF)
        refs[-1][...] = summed(refs[count : 2 * count]).astype(BF)

    def spec(array, flip):
        if array.ndim == 3:
            return pl.BlockSpec((None, rows, cols), lambda i, s: (0, s[which] ^ flip, 0))
        return pl.BlockSpec((rows, cols), lambda i, s: (s[which] ^ flip, 0))

    out = pl.BlockSpec((rows, cols), lambda i, s: (0, 0))
    shape = jax.ShapeDtypeStruct((rows, cols), BF)
    return pick_call(
        body, place, tuple(parts) * 2, [spec(p, 1) for p in parts] + [spec(p, 0) for p in parts],
        (shape, shape), (out, out), (1,), "settle", deps, (), cost,
    )


def mirror(place, kept, got, deps):
    _, rows, half = kept.shape

    def body(s, a, b, out):
        out[...] = (a[...].astype(F32) + b[...].astype(F32)).astype(BF)

    spec = pl.BlockSpec((None, rows, half), lambda i, s: (1, 0, 0))
    return pick_call(
        body, place, (kept, got), [spec, spec], jax.ShapeDtypeStruct((rows, half), BF),
        pl.BlockSpec((rows, half), lambda i, s: (0, 0)), (1,), "mirror", deps,
    )


def spread(place, pairs, extra, deps):
    nz, _, half = pairs[0][0].shape
    arrays = tuple(v for pair in pairs for v in pair) + tuple(extra)
    rows = sum(kept.shape[1] for kept, got in pairs) + (extra[0].shape[0] if extra else 0)

    def body(s, *refs):
        for step in range(nz):
            block = lax.rem(s[2] + step, nz)
            out = refs[len(arrays) + step]
            at = 0
            for p in range(len(pairs)):
                a, b = refs[2 * p], refs[2 * p + 1]
                r = a.shape[1]
                total = a[block].astype(F32) + b[block].astype(F32)
                out[at : at + r] = total.astype(out.dtype)
                at += r
            if extra:
                came = take_table(refs[2 * len(pairs) - 1], nz, refs[1].shape[1] // 2)
                total = refs[2 * len(pairs)][...].astype(F32) + came.astype(F32)
                out[at:] = total.astype(out.dtype)

    whole = lambda array: pl.BlockSpec(array.shape, lambda i, s: (0,) * array.ndim)
    shapes = [jax.ShapeDtypeStruct((rows, half), F32)]
    shapes += [jax.ShapeDtypeStruct((rows, half), BF)] * (nz - 1)
    out = pl.BlockSpec((rows, half), lambda i, s: (0, 0))
    return pick_call(
        body, place, arrays, [whole(a) for a in arrays], tuple(shapes), (out,) * nz,
        (1,), "spread", deps,
    )


def finish(place, parts, cuts, vectors, deps, cost=None):
    half = parts[0].shape[-1]
    count = len(parts)
    taken = sum(rows * wide for rows, wide in cuts)
    table = parts[0].shape[-2] - taken

    def body(s, *refs):
        outs = refs[count:]
        at = 0
        for (rows, wide), out in zip(cuts, outs):
            for j in range(wide):
                lo = at + j * rows
                total = refs[0][lo : lo + rows].astype(F32)
                for ref in refs[1:count]:
                    total = total + ref[lo : lo + rows].astype(F32)
                out[:, j * half : (j + 1) * half] = total
            at += rows * wide
        if vectors:
            sums = refs[-1]
            total = refs[0][at:].astype(F32)
            for ref in refs[1:count]:
                total = total + ref[at:].astype(F32)
            sums[...] = total
            for (rows, where, length), out in zip(vectors, outs[len(cuts) :]):
                for k in range(rows):
                    row, col = where(s, k)
                    line = sums[pl.ds(row, 1), :]
                    line = pltpu.roll(line, lax.rem(half - col, half), 1)
                    out[k : k + 1, :] = line[:, :length]

    whole = lambda shape: pl.BlockSpec(shape, lambda i, s: (0, 0))
    first = lambda shape: (
        whole(shape) if len(shape) == 2 else pl.BlockSpec((None,) + shape[1:], lambda i, s: (0, 0, 0))
    )
    shapes = [(rows, wide * half) for rows, wide in cuts]
    shapes += [(rows, length) for rows, where, length in vectors]
    scratch = [pltpu.VMEM((table, half), F32)] if vectors else []
    return pick_call(
        body, place, tuple(parts), [first(p.shape) for p in parts],
        tuple(jax.ShapeDtypeStruct(shape, F32) for shape in shapes),
        tuple(whole(shape) for shape in shapes), (1,), "finish", deps, scratch, cost,
    )


def along_z(place, pairs, extra, deps, cost=None):
    if pairs[0][0].shape[0] == 4:
        give, keep = fold(place, pairs, extra, deps, cost)
        return (keep, to_z_pair(give))
    blocks = spread(place, pairs, extra, deps)
    return (blocks[0],) + tuple(to_z(b, step + 1) for step, b in enumerate(blocks[1:]))


def across_z(state):
    if state[0].ndim == 3:
        give = (state[0][1].astype(F32) + state[1][1].astype(F32)).astype(BF)
        return state + (to_z_mirror(give),), give
    return state, state[0]


def local(
    patches, cotangent, image_quads, keep_pick, image_gsd,
    enc_gains, enc_biases, enc_qkv, enc_proj, enc_fc1, enc_fc1_bias, enc_fc2,
    dec_embed, dec_gains, dec_biases, dec_qkv, dec_proj, dec_fc1, dec_fc1_bias, dec_fc2,
):
    d = lax.axis_index("dp")
    y = lax.axis_index("segment")
    count = lax.axis_size("dp")
    c, x, z = d & 1, (d >> 1) & 1, d >> 2
    nzx = count // 2
    nz = nzx // 2
    info = jnp.stack([y, c, x]).astype(I32)
    place = jnp.stack([x, y, z, d]).astype(I32)
    other_x, other_y = (1 - x).reshape(1), (1 - y).reshape(1)
    own_c, other_c = c.reshape(1), (1 - c).reshape(1)
    row_x = patches[0]
    row_cot = cotangent[0]
    d_enc, d_dec = enc_gains.shape[1], dec_gains.shape[1]
    f_enc, f_dec = enc_fc1.shape[1], dec_fc1.shape[1]
    r_h, r_d = f_enc // count, d_enc // count
    s_d, s_h = d_dec // count, f_dec // count
    split = lambda v: v.reshape((nz, 2) + v.shape[1:])

    act, xs, xk, hs, hk, packed, lse, mixed, resid, slope = enc_forward(
        info, image_quads, row_x, enc_gains, enc_biases, enc_fc1_bias[None, :],
        enc_qkv, enc_proj, enc_fc1, enc_fc2, nzx,
    )
    xr = to_core(xs)
    hids = (hk, to_x(hs), to_y(hk), to_corner(hs))
    dact, dh_own, dh_other, dec_give, dec_keep, dec_small = decoder(
        info, image_quads, image_gsd, keep_pick, act, row_cot, dec_gains, dec_biases,
        dec_fc1_bias[None, :], dec_embed, dec_qkv, dec_proj, dec_fc1, dec_fc2, nzx,
    )
    dec_got = to_core(dec_give)
    dys = (dh_own, to_x(dh_own), to_y(dh_other), to_corner(dh_other))
    du, dres, small_a = enc_ffn_back(
        dact, resid, slope, enc_gains, enc_fc1, enc_fc2, (xr,) + hids[1:]
    )
    dur = to_core(du)
    if nz == 4:
        block = (nz, 4 * dec_keep.shape[2], dec_keep.shape[3])
        d_give, d_keep = fold_wide(place, dec_keep.reshape(block), dec_got.reshape(block), (du,))
        d_got = to_z_pair(d_give)
    else:
        block = (nz, 2, 2 * dec_keep.shape[2], dec_keep.shape[3])
        d_give, d_keep = turn(
            place, ((dec_keep.reshape(block), dec_got.reshape(block), 0),), (), (du,)
        )
        d_got = to_x(d_give)
    w_give = down_grad(other_c, hids, dys, (d_keep,))
    w_got = to_core(w_give)
    f_give = up_grad(other_y, xk, xr, du, dur, (w_give,))
    f_got = to_y(f_give)
    if nz == 4:
        w_give, w_keep = down_fold(place, hids, dys, w_got, (f_give,))
        w_z = (w_keep, to_z_pair(w_give))
    else:
        w_keep = down_grad(own_c, hids, dys, (f_give,))
        w_z = along_z(place, ((w_keep, w_got),), (), ())
    dx, dp, dp_one = enc_att_back(
        info, image_quads, row_x, du, dres, packed, lse, mixed, enc_gains, small_a, dec_small,
        enc_qkv, enc_proj, (w_z[0],),
    )
    dp_oner = to_core(dp_one)
    dpr = to_core(dp)
    if nz == 4:
        dec_z, last_d = across_z((d_keep, d_got))
    else:
        halves = (nz, 2, d_keep.shape[1] // 2, d_keep.shape[2])
        d_give, d_keep = turn(
            place, ((d_keep.reshape(halves), d_got.reshape(halves), 1),), (), (dx,)
        )
        last_d = d_keep
        dec_z = along_z(place, ((d_keep, to_y(d_give)),), (), ())
    ta_give = qk_grad(other_x, xk, xr, dp, dpr, (dx, last_d))
    ta_got = to_x(ta_give)
    tb_give, table = vo_grad(other_y, xk, xr, dp_one, dp_oner, du, dur, (ta_give,))
    tb_got = to_y(tb_give)
    f_give, f_keep = up_turn(place, xk, xr, du, dur, f_got, (table,))
    f_got = to_x(f_give)
    ta_give, ta_keep = qk_turn(place, xk, xr, dp, dpr, ta_got, (f_keep,))
    ta_got = to_y(ta_give)
    last = ta_keep
    if nz == 4:
        d_give, d_keep = settle(place, dec_z, 0, (last,), REST)
        d_got = to_x(d_give)
        last = d_keep
    tb_give, tb_keep, table = vo_turn(
        place, xk, xr, dp_one, dp_oner, du, dur, tb_got, table, (last,)
    )
    tb_got = to_x(tb_give)
    f_z = along_z(place, ((f_keep, f_got),), (), (tb_keep,), MORE)
    last = f_z[0]
    if nz == 4:
        give = mirror(place, w_z[0], w_z[1], (last,))
        w_z = w_z + (to_z_mirror(give),)
        last = give
    att_z = along_z(place, ((ta_keep, ta_got), (tb_keep, tb_got)), (table,), (last,))
    last = att_z[0]
    if nz == 4:
        d_give, d_keep = settle(place, (d_keep, d_got), 1, (last,))
        dec_z = (d_keep, to_y(d_give))
        last = d_keep
    (g_fc2,) = finish(place, w_z, ((r_h, 1),), (), (last,))
    last = g_fc2
    f_z, last_f = across_z(f_z)
    if len(att_z) == 2:
        give = mirror(place, att_z[0], att_z[1], (last_f, last))
        att_z = att_z + (to_z_mirror(give),)
        last = give
    h_emb, h_qkv, h_proj, h_fc1, h_fc2 = finish(
        place, dec_z, ((r_d, 1), (s_d, 3), (s_d, 1), (s_d, s_h // s_d), (s_h, 1)), (),
        (last,),
    )
    (g_fc1,) = finish(place, f_z, ((r_d, r_h // r_d),), (), (h_fc2,), SOME)

    piece, lanes = row_x.shape[0], TABLE // 2

    def spot(base, row, col):
        line = base + (col // piece) * 16 + row
        return lax.rem(line, lanes), (line // lanes) * piece + lax.rem(col, piece)

    def window(base, first, per_y, length):
        return lambda s, k: spot(base, first + s[1] * per_y + k, s[3] * length)

    def window_flat(base, first, wide, length):
        def where(s, k):
            col = (s[1] * count + s[3]) * length
            return spot(base, first + col // wide, lax.rem(col, wide))

        return where

    base = d_enc // piece * 16
    v_h, u_h = f_enc // (2 * count), f_dec // (2 * count)
    vectors = (
        (1, window(0, 0, 1, r_d), r_d),
        (3, window(0, 2, 3, r_d), r_d),
        (1, window_flat(0, 8, d_enc, v_h), v_h),
        (1, window(base, 0, 1, s_d), s_d),
        (4, window(base, 2, 4, s_d), s_d),
        (1, window_flat(base, 10, d_dec, u_h), u_h),
    )
    g_qkv, g_proj, e_gains, e_biases, e_up, d_gains, d_biases, d_up = finish(
        place, att_z, ((r_d, 3), (r_d, 1)), vectors, ()
    )
    return (
        dx[None], e_gains, e_biases, g_qkv, g_proj, g_fc1, e_up.reshape(-1), g_fc2,
        h_emb, d_gains, d_biases, h_qkv, h_proj, h_fc1, d_up.reshape(-1), h_fc2,
    )


def solution(mesh):
    rows3 = P("segment", "dp", None)
    placed = (rows3, rows3, P(None, "dp", None), P(None, "dp"), P(None, "dp", None)) + (P(),) * 15
    both, wide, flat = P("segment", "dp"), P("dp", "segment"), P(("segment", "dp"))
    return jax.shard_map(
        local,
        mesh=mesh,
        in_specs=placed,
        out_specs=(
            rows3, both, both, wide, wide, wide, flat, wide,
            wide, both, both, wide, wide, wide, flat, wide,
        ),
        check_vma=False,
    )
```

```python
import functools
import math

import jax
import jax.numpy as jnp
import numpy as np
from jax import lax
from jax.experimental import pallas as pl
from jax.experimental.pallas import tpu as pltpu
from jax.sharding import PartitionSpec as P

BF, F32, I32 = jnp.bfloat16, jnp.float32, jnp.int32
HEADS = 16
EPSILON = 1e-06
LOG2E = 1.4426950408889634
LN2 = 0.6931471805599453
FAR = -1e30
TABLE = 96
VMEM_LIMIT = 60 * 1024 * 1024
SOME = pl.CostEstimate(flops=4000000000, bytes_accessed=10**6, transcendentals=0)
MORE = pl.CostEstimate(flops=8 * 10**9, bytes_accessed=10**6, transcendentals=0)
WAIT = pl.CostEstimate(flops=12 * 10**9, bytes_accessed=10**6, transcendentals=0)
REST = pl.CostEstimate(flops=6 * 10**9, bytes_accessed=10**6, transcendentals=0)
LONGER = pl.CostEstimate(flops=2 * 10**11, bytes_accessed=10**8, transcendentals=0)
LONG = pl.CostEstimate(flops=3 * 10**10, bytes_accessed=10**8, transcendentals=0)
TINY = pl.CostEstimate(flops=1000, bytes_accessed=1000, transcendentals=0)
ANY = pl.BlockSpec(memory_space=pl.ANY)
VM = pl.BlockSpec(memory_space=pltpu.VMEM)
SM = pl.BlockSpec(memory_space=pltpu.SMEM)


def dot(a, b, ca, cb):
    return lax.dot_general(a, b, (((ca,), (cb,)), ((), ())), preferred_element_type=F32)


def norm_parts(v):
    c = v - jnp.mean(v, -1, keepdims=True)
    r = lax.rsqrt(jnp.mean(c * c, -1, keepdims=True) + EPSILON)
    return c * r, r


def norm_back(v, gain, e):
    n, r = norm_parts(v)
    eg = e * gain
    dv = r * (eg - jnp.mean(eg, -1, keepdims=True) - n * jnp.mean(eg * n, -1, keepdims=True))
    return dv, jnp.sum(e * n, 0, keepdims=True), jnp.sum(e, 0, keepdims=True)


def gelu_parts(u):
    size = jnp.abs(u)
    t = 1.0 / (1.0 + 0.2316419 * size)
    bell = jnp.exp2(u * u * (-0.5 * LOG2E))
    poly = 1.330274429 * t - 1.821255978
    poly = poly * t + 1.781477937
    poly = poly * t - 0.356563782
    poly = poly * t + 0.319381530
    dens = bell * 0.3989422804014327
    tail = poly * t * dens
    cdf = jnp.where(u >= 0.0, 1.0 - tail, tail)
    return u * cdf, cdf + u * dens


def three(v):
    hi = v.astype(BF)
    rest = v - hi.astype(F32)
    mid = rest.astype(BF)
    low = (rest - mid.astype(F32)).astype(BF)
    return hi.astype(F32), mid.astype(F32), low.astype(F32)


def stack16(rows, width):
    at = lax.broadcasted_iota(I32, (16, width), 0)
    out = jnp.zeros((16, width), F32)
    for i, row in rows:
        out = jnp.where(at == i, row, out)
    return out


def image_codes(quads, sizes_ref, m, images):
    end = 0
    img = jnp.zeros(quads.shape, I32)
    first = jnp.zeros(quads.shape, I32)
    for k in range(images):
        end = end + sizes_ref[m, 0, k]
        over = quads >= end
        img = img + over.astype(I32)
        first = jnp.where(over, end, first)
    return img, first


def mask_rows(img, images, width):
    at = lax.broadcasted_iota(I32, (16, width), 0)
    same = at == img
    inside = at < images
    q_rows = jnp.where(inside & same, 1.0, 0.0)
    k_rows = jnp.where(inside & jnp.logical_not(same), FAR, 0.0)
    k_rows = jnp.where((at >= images) & (at < images + 3), 1.0, k_rows)
    return q_rows, k_rows


def attend_forward(packed, mixed, lse, q_rows, k_rows, h, width, dh, cols, images):
    q = packed[pl.ds(pl.multiple_of(h * dh, dh), dh), cols]
    k = packed[pl.ds(pl.multiple_of(width + h * dh, dh), dh), cols]
    v = packed[pl.ds(pl.multiple_of(2 * width + h * dh, dh), dh), cols]
    qa = jnp.concatenate([q, q_rows[:, cols]], 0)
    ka = jnp.concatenate([k, k_rows[:, cols]], 0)
    s = dot(ka, qa, 0, 0)
    top = jnp.max(s, 0, keepdims=True)
    e = jnp.exp2(s - top).astype(BF)
    va = jnp.concatenate([v, jnp.ones((16, v.shape[1]), BF)], 0)
    o = dot(va, e, 1, 0)
    total = o[dh : dh + 1]
    mixed[pl.ds(pl.multiple_of(h * dh, dh), dh), cols] = (o[:dh] / total).astype(BF)
    lse[pl.ds(h, 1), cols] = top + jnp.log2(total)


def attend_backward(
    packed, mixed, lse, d_mixed, d_packed, q_rows, k_rows, h, width, dh, cols, images
):
    rows = [pl.ds(pl.multiple_of(part * width + h * dh, dh), dh) for part in range(3)]
    q, k, v = (packed[r, cols] for r in rows)
    count = q.shape[1]
    neg = three(-lse[pl.ds(h, 1), cols])
    extra = stack16([(images + i, neg[i]) for i in range(3)], count)
    qa = jnp.concatenate([q, (q_rows[:, cols].astype(F32) + extra).astype(BF)], 0)
    ka = jnp.concatenate([k, k_rows[:, cols]], 0)
    p = jnp.exp2(dot(ka, qa, 0, 0))
    do = d_mixed[rows[0], cols]
    centre = jnp.sum(do.astype(F32) * mixed[rows[0], cols].astype(F32), 0, keepdims=True)
    neg = three(-centre)
    da = jnp.concatenate([do, stack16([(i, neg[i]) for i in range(3)], count).astype(BF)], 0)
    at = lax.broadcasted_iota(I32, (16, count), 0)
    va = jnp.concatenate([v, jnp.where(at < 3, 1.0, 0.0).astype(BF)], 0)
    ds = (p * dot(va, da, 0, 0)).astype(BF)
    dv = dot(do, p.astype(BF), 1, 1)
    dk = dot(q, ds, 1, 1) * LN2
    dq = dot(k, ds, 1, 0) * (dh**-0.5)
    d_packed[rows[0], cols] = dq.astype(BF)
    d_packed[rows[1], cols] = dk.astype(BF)
    d_packed[rows[2], cols] = dv.astype(BF)


def attend_forward_kept(packed, mixed, scale, kept, q_rows, k_rows, h, side, width, dh, cols):
    q = packed[pl.ds(pl.multiple_of(h * dh, dh), dh), cols]
    k = packed[pl.ds(pl.multiple_of(width + h * dh, dh), dh), cols]
    v = packed[pl.ds(pl.multiple_of(2 * width + h * dh, dh), dh), cols]
    qa = jnp.concatenate([q, q_rows[:, cols]], 0)
    ka = jnp.concatenate([k, k_rows[:, cols]], 0)
    s = dot(ka, qa, 0, 0)
    top = jnp.max(s, 0, keepdims=True)
    e = jnp.exp2(s - top).astype(BF)
    kept[2 * h + side] = e
    va = jnp.concatenate([v, jnp.ones((16, v.shape[1]), BF)], 0)
    o = dot(va, e, 1, 0)
    part = 1.0 / o[dh : dh + 1]
    mixed[pl.ds(pl.multiple_of(h * dh, dh), dh), cols] = (o[:dh] * part).astype(BF)
    scale[pl.ds(h, 1), cols] = part


def attend_backward_kept(packed, mixed, scale, kept, d_mixed, h, width, dh, sides):
    rows = [pl.ds(pl.multiple_of(part * width + h * dh, dh), dh) for part in range(3)]
    read = [[packed[r, cols] for r in rows] for cols in sides]
    grads = []
    for side, cols in enumerate(sides):
        q, k, v = read[side]
        count = q.shape[1]
        part = scale[pl.ds(h, 1), cols]
        do = d_mixed[rows[0], cols].astype(F32) * part
        centre = jnp.sum(do * mixed[rows[0], cols].astype(F32), 0, keepdims=True)
        do = do.astype(BF)
        neg = three(-centre)
        da = jnp.concatenate([do, stack16([(i, neg[i]) for i in range(3)], count).astype(BF)], 0)
        at = lax.broadcasted_iota(I32, (16, count), 0)
        va = jnp.concatenate([v, jnp.where(at < 3, 1.0, 0.0).astype(BF)], 0)
        e = kept[2 * h + side]
        ds = (e.astype(F32) * dot(va, da, 0, 0)).astype(BF)
        dv = dot(e, do.T, 1, 0).T
        dk = dot(ds, q.T, 1, 0).T * LN2
        dq = dot(k, ds, 1, 0) * (dh**-0.5)
        grads.append((dq, dk, dv))
    for cols, parts in zip(sides, grads):
        for r, part in zip(rows, parts):
            packed[r, cols] = part.astype(BF)


def enc_forward_kernel(
    info, sizes, x_ref, gains, biases, up_bias, wqkv_h, wo_h, w1_h, w2_h,
    out_ref, xs_h, xk_h, hs_h, hk_h, packed_h, lse, mixed_h, resid_h, slope_h,
    wqkv, wo, w1, w2, packed, mixed, resid, slope, xt, ht, n2_s, acc, qr, kr, sems,
):
    m, c, x = info[0], info[1], info[2]
    images = sizes.shape[2]
    tokens, width = x_ref.shape
    hidden = w1.shape[1]
    dh = width // HEADS
    nzx = xt.shape[1]
    r_d = width // (2 * nzx)
    r_h = hidden // (2 * nzx)
    tile = 512
    copies = [pltpu.make_async_copy(wqkv_h, wqkv, sems.at[0])]
    copies.append(pltpu.make_async_copy(wo_h, wo, sems.at[1]))
    copies.append(pltpu.make_async_copy(w1_h, w1, sems.at[2]))
    copies.append(pltpu.make_async_copy(w2_h, w2, sems.at[3]))
    for copy in copies:
        copy.start()
    gain = gains[...].astype(F32)
    bias = biases[...].astype(F32)

    def keep_rows(values, start):
        for a in range(nzx):
            for cc in range(2):
                at = (a * 2 + cc) * r_d
                xt[cc, a, start : start + r_d, :] = values[at : at + r_d]

    quads = lax.broadcasted_iota(I32, (1, tokens), 1)
    img, _ = image_codes(quads, sizes, m, images)
    q_rows, k_rows = mask_rows(img, images, tokens)
    qr[...] = q_rows.astype(BF)
    kr[...] = k_rows.astype(BF)
    n, _ = norm_parts(x_ref[...].astype(F32))
    n1 = (n * gain[0:1] + bias[0:1]).astype(BF)
    keep_rows(n1.T, 0)
    copies[0].wait()
    for part in range(3):
        cols = slice(part * width, (part + 1) * width)
        got = dot(n1, wqkv[:, cols], 1, 0)
        if part == 0:
            got = (got + bias[1:2]) * (dh**-0.5 * LOG2E)
        if part == 2:
            got = got + bias[2:3]
        packed[cols, :] = got.astype(BF).T

    def head(h, carry):
        attend_forward(packed, mixed, lse, qr, kr, h, width, dh, slice(0, tokens), images)
        return carry

    lax.fori_loop(0, HEADS, head, 0, unroll=4)
    outs = [pltpu.make_async_copy(packed, packed_h, sems.at[4])]
    outs.append(pltpu.make_async_copy(mixed, mixed_h, sems.at[5]))
    for copy in outs:
        copy.start()
    mix = mixed[...]
    keep_rows(mix, r_d)
    copies[1].wait()
    res = x_ref[...].astype(F32) + dot(mix, wo[...], 0, 0) + bias[3:4]
    resid[...] = res
    n, _ = norm_parts(res)
    n2 = (n * gain[1:2] + bias[4:5]).astype(BF)
    n2_s[...] = n2
    keep_rows(n2.T, 2 * r_d)
    more = [
        pltpu.make_async_copy(resid, resid_h, sems.at[6]),
        pltpu.make_async_copy(xt.at[1 - c], xs_h, sems.at[7]),
        pltpu.make_async_copy(xt.at[c], xk_h, sems.at[8]),
    ]
    for copy in more:
        copy.start()
    outs = outs + more
    acc[...] = res + bias[5:6]
    copies[2].wait()
    copies[3].wait()
    per = tile // (2 * r_h)

    def ffn(t, carry):
        cols = pl.ds(pl.multiple_of(t * tile, tile), tile)
        u = dot(n2_s[...], w1[:, cols], 1, 0) + up_bias[:, cols].astype(F32)
        hid, dif = gelu_parts(u)
        hid = hid.astype(BF)
        slope[:, cols] = dif.astype(BF)
        hid_t = hid.T
        for a in range(per):
            for cc in range(2):
                at = (a * 2 + cc) * r_h
                zx = t * per + a
                ht[zx & 1, zx >> 1, cc, :, :] = hid_t[at : at + r_h]
        acc[...] += dot(hid, w2[cols, :], 1, 0)
        return carry

    lax.fori_loop(0, hidden // tile, ffn, 0)
    out_ref[...] = acc[...].astype(BF)
    more = [
        pltpu.make_async_copy(ht.at[1 - x], hs_h, sems.at[2]),
        pltpu.make_async_copy(ht.at[x], hk_h, sems.at[3]),
        pltpu.make_async_copy(slope, slope_h, sems.at[9]),
    ]
    for copy in more:
        copy.start()
    for copy in outs + more:
        copy.wait()


def enc_forward(info, sizes, x, gains, biases, up_bias, wqkv, wo, w1, w2, nzx):
    tokens, width = x.shape
    hidden = w1.shape[1]
    rows = 3 * width // (2 * nzx)
    half = jax.ShapeDtypeStruct((nzx, rows, tokens), BF)
    h_shape = (nzx // 2, 2, hidden // (2 * nzx), tokens)
    h_half = jax.ShapeDtypeStruct(h_shape, BF)
    return pl.pallas_call(
        enc_forward_kernel,
        out_shape=(
            jax.ShapeDtypeStruct((tokens, width), BF),
            half,
            half,
            h_half,
            h_half,
            jax.ShapeDtypeStruct((3 * width, tokens), BF),
            jax.ShapeDtypeStruct((HEADS, tokens), F32),
            jax.ShapeDtypeStruct((width, tokens), BF),
            jax.ShapeDtypeStruct((tokens, width), F32),
            jax.ShapeDtypeStruct((tokens, hidden), BF),
        ),
        in_specs=[SM, SM, VM, VM, VM, VM, ANY, ANY, ANY, ANY],
        out_specs=(VM, ANY, ANY, ANY, ANY, ANY, VM, ANY, ANY, ANY),
        scratch_shapes=[
            pltpu.VMEM(wqkv.shape, BF),
            pltpu.VMEM(wo.shape, BF),
            pltpu.VMEM(w1.shape, BF),
            pltpu.VMEM(w2.shape, BF),
            pltpu.VMEM((3 * width, tokens), BF),
            pltpu.VMEM((width, tokens), BF),
            pltpu.VMEM((tokens, width), F32),
            pltpu.VMEM((tokens, hidden), BF),
            pltpu.VMEM((2, nzx, rows, tokens), BF),
            pltpu.VMEM((2,) + h_shape, BF),
            pltpu.VMEM((tokens, width), BF),
            pltpu.VMEM((tokens, width), F32),
            pltpu.VMEM((16, tokens), BF),
            pltpu.VMEM((16, tokens), BF),
            pltpu.SemaphoreType.DMA((10,)),
        ],
        compiler_params=pltpu.CompilerParams(vmem_limit_bytes=VMEM_LIMIT),
        cost_estimate=TINY,
        name="enc_forward",
    )(info, sizes, x, gains, biases, up_bias, wqkv, wo, w1, w2)


def enc_ffn_back_kernel(
    dy_ref, resid, slope, gains, w1_h, w2_h, *rest
):
    du_ref, dres, small, w1, w2, acc, sems = rest[-7:]
    tokens, width = dy_ref.shape
    hidden = w1.shape[1]
    tile = 512
    parts = hidden // tile
    loads = []
    for t in range(parts):
        at = pl.ds(t * tile, tile)
        loads.append(pltpu.make_async_copy(w2_h.at[at, :], w2.at[at, :], sems.at[2 * t]))
        loads.append(pltpu.make_async_copy(w1_h.at[:, at], w1.at[:, at], sems.at[2 * t + 1]))
    for copy in loads:
        copy.start()
    gain = gains[...].astype(F32)
    dy = dy_ref[...]
    total = jnp.zeros((tokens, width), F32)
    acc[...] = total
    small[...] = jnp.zeros(small.shape, F32)
    for t in range(parts):
        loads[2 * t].wait()
        loads[2 * t + 1].wait()
        cols = slice(t * tile, (t + 1) * tile)
        dh = dot(dy, w2[cols, :], 1, 1)
        du = (dh * slope[:, cols].astype(F32)).astype(BF)
        du_ref[:, cols] = du
        sums = jnp.sum(du.astype(F32), 0, keepdims=True)
        row, col = divmod(t * tile, width)
        small[8 + row : 9 + row, col : col + tile] = sums
        acc[...] += dot(du, w1[:, cols], 1, 1)
    dv, d_gain, d_shift = norm_back(resid[...], gain[1:2], acc[...])
    dyf = dy.astype(F32)
    res = dyf + dv
    dres[...] = res
    da = res.astype(BF)
    du_ref[:, hidden:] = da
    small[1:2, :] = d_gain
    small[5:6, :] = jnp.sum(da.astype(F32), 0, keepdims=True)
    small[6:7, :] = d_shift
    small[7:8, :] = jnp.sum(dyf, 0, keepdims=True)


def enc_ffn_back(dy, resid, slope, gains, w1, w2, deps):
    tokens, width = dy.shape
    hidden = w1.shape[1]
    return pl.pallas_call(
        enc_ffn_back_kernel,
        out_shape=(
            jax.ShapeDtypeStruct((tokens, hidden + width), BF),
            jax.ShapeDtypeStruct((tokens, width), F32),
            jax.ShapeDtypeStruct((16, width), F32),
        ),
        in_specs=[VM, VM, VM, VM] + [ANY] * (2 + len(deps)),
        out_specs=(VM, VM, VM),
        scratch_shapes=[
            pltpu.VMEM(w1.shape, BF),
            pltpu.VMEM(w2.shape, BF),
            pltpu.VMEM((tokens, width), F32),
            pltpu.SemaphoreType.DMA((2 * (hidden // 512),)),
        ],
        compiler_params=pltpu.CompilerParams(vmem_limit_bytes=VMEM_LIMIT),
        cost_estimate=LONGER,
        name="enc_ffn_back",
    )(dy, resid, slope, gains, w1, w2, *deps)


def enc_att_back_kernel(
    info, sizes, x_ref, da_h, dres, packed, lse, mixed, gains, small_a, small_d, wqkv_h, wo_h, *rest
):
    dx_ref, d_two, d_one, wqkv, wo, da, d_mixed, d_packed, qr, kr, sems = rest[-11:]
    m = info[0]
    images = sizes.shape[2]
    tokens, width = x_ref.shape
    dh = width // HEADS
    loads = [
        pltpu.make_async_copy(wo_h, wo, sems.at[0]),
        pltpu.make_async_copy(wqkv_h, wqkv, sems.at[1]),
        pltpu.make_async_copy(da_h.at[:, pl.ds(da_h.shape[1] - width, width)], da, sems.at[2]),
    ]
    for copy in loads:
        copy.start()
    gain = gains[...].astype(F32)
    quads = lax.broadcasted_iota(I32, (1, tokens), 1)
    img, _ = image_codes(quads, sizes, m, images)
    q_rows, k_rows = mask_rows(img, images, tokens)
    qr[...] = q_rows.astype(BF)
    kr[...] = k_rows.astype(BF)
    loads[0].wait()
    loads[2].wait()
    d_mixed[...] = dot(wo[...], da[...], 1, 1).astype(BF)

    def head(h, carry):
        attend_backward(
            packed, mixed, lse, d_mixed, d_packed, qr, kr, h, width, dh, slice(0, tokens), images
        )
        return carry

    lax.fori_loop(0, HEADS, head, 0, unroll=4)
    loads[1].wait()
    dp = d_packed[...]
    part = width // 2
    for half in range(2):
        for j in range(2):
            at, to = (half * 3 + j) * part, (half * 2 + j) * part
            d_two[to : to + part, :] = dp[at : at + part]
        at = (half * 3 + 2) * part
        d_one[half * part : (half + 1) * part, :] = dp[at : at + part]
    table = d_one.shape[0] - TABLE
    d_one[width:table, :] = jnp.zeros((table - width, tokens), BF)
    e = dot(wqkv[...], dp, 1, 0).T
    dv, d_gain, d_shift = norm_back(x_ref[...].astype(F32), gain[0:1], e)
    dx_ref[...] = (dres[...] + dv).astype(BF)
    ones = jnp.ones((16, tokens), BF)
    sums = dot(ones, dp, 1, 1)
    mine = {0: d_gain, 2: d_shift, 3: sums[0:1, :width], 4: sums[0:1, 2 * width :]}
    rows = [mine[i] if i in mine else small_a[i : i + 1, :] for i in range(16)]
    rows = jnp.concatenate(rows, 0).astype(BF)
    piece = tokens
    for p in range(width // piece):
        at = table + p * 16
        d_one[at : at + 16, :] = rows[:, p * piece : (p + 1) * piece]
    rows = small_d[...].astype(BF)
    for p in range(rows.shape[1] // piece):
        at = table + (width // piece + p) * 16
        d_one[at : at + 16, :] = rows[:, p * piece : (p + 1) * piece]


def enc_att_back(
    info, sizes, x, da, dres, packed, lse, mixed, gains, small_a, small_d, wqkv, wo, deps
):
    tokens, width = x.shape
    return pl.pallas_call(
        enc_att_back_kernel,
        out_shape=(
            jax.ShapeDtypeStruct((tokens, width), BF),
            jax.ShapeDtypeStruct((2 * width, tokens), BF),
            jax.ShapeDtypeStruct(((width // TABLE + 2) * TABLE, tokens), BF),
        ),
        in_specs=[SM, SM, VM, ANY] + [VM] * 7 + [ANY] * (2 + len(deps)),
        out_specs=(VM, VM, VM),
        scratch_shapes=[
            pltpu.VMEM(wqkv.shape, BF),
            pltpu.VMEM(wo.shape, BF),
            pltpu.VMEM((tokens, width), BF),
            pltpu.VMEM((width, tokens), BF),
            pltpu.VMEM((3 * width, tokens), BF),
            pltpu.VMEM((16, tokens), BF),
            pltpu.VMEM((16, tokens), BF),
            pltpu.SemaphoreType.DMA((3,)),
        ],
        compiler_params=pltpu.CompilerParams(vmem_limit_bytes=VMEM_LIMIT),
        cost_estimate=TINY,
        name="enc_att_back",
    )(info, sizes, x, da, dres, packed, lse, mixed, gains, small_a, small_d, wqkv, wo, *deps)


def wave_codes(phases):
    turn = jnp.floor(phases * 0.6366197723675814 + 0.5)
    r = phases - turn * 1.5703125
    r = r - turn * 4.837512969970703125e-4
    r = r - turn * 7.54978995489188216e-8
    sq = r * r
    sn = -1.9515295891e-4 * sq + 8.3321608736e-3
    sn = (sn * sq - 1.6666654611e-1) * sq * r + r
    cs = 2.443315711809948e-5 * sq - 1.388731625493765e-3
    cs = (cs * sq + 4.166664568298827e-2) * sq * sq - 0.5 * sq + 1.0
    quarter = turn.astype(I32) & 3
    odd = (quarter & 1) == 1
    sine = jnp.where(odd, cs, sn)
    cosine = jnp.where(odd, sn, cs)
    sine = jnp.where(quarter >= 2, -sine, sine)
    cosine = jnp.where((quarter == 1) | (quarter == 2), -cosine, cosine)
    return sine, cosine


def decoder_kernel(
    info, sizes, gsd, pick_ref, freq, act_ref, cot_ref, gains, biases, up_bias,
    wemb, wqkv, wo_h, w1_h, w2_h,
    dact_ref, dh_own, dh_other, gs_h, gk_h, small,
    x_s, n_s, packed, mixed, scale, res_s, n2_s, hid_s, du_s, cot_s, dmix, kept, emb_s, demb_s,
    grads, wo, w1, w2, qr, kr, sems,
):
    m, c = info[0], info[1]
    loads = [
        pltpu.make_async_copy(wo_h, wo, sems.at[4]),
        pltpu.make_async_copy(w1_h, w1, sems.at[5]),
        pltpu.make_async_copy(w2_h, w2, sems.at[6]),
    ]
    for copy in loads:
        copy.start()
    images = sizes.shape[2]
    quads, e_width = act_ref.shape
    slots, width = cot_ref.shape
    hidden = w1.shape[1]
    dh = width // HEADS
    chunk = 512
    parts = slots // chunk
    nzx = grads.shape[1]
    half = width // 2
    gain = gains[...].astype(F32)
    bias = biases[...].astype(F32)

    start, best, seen = 0, 0, 0
    for k in range(images):
        size = sizes[m, 0, k]
        start = jnp.where(size > best, seen, start)
        best = jnp.maximum(size, best)
        seen = seen + size

    lane = lax.broadcasted_iota(I32, (1, slots), 1)
    img, _ = image_codes(((lane + 4 * start) & (slots - 1)) >> 2, sizes, m, images)
    q_rows, k_rows = mask_rows(img, images, slots)
    qr[...] = q_rows.astype(BF)
    kr[...] = k_rows.astype(BF)
    emb = dot(act_ref[...], wemb[...], 1, 0) + bias[6:7]
    hi = emb.astype(BF)
    emb_s[0] = hi
    emb_s[1] = (emb - hi.astype(F32)).astype(BF)
    picks = pick_ref[pl.ds(m, 1), :]

    def slot_of(i, count):
        row = lax.broadcasted_iota(I32, (chunk, count), 0) + i * chunk
        return (row + 4 * start) & (slots - 1)

    def shown(i):
        slot = slot_of(i, quads)
        col = lax.broadcasted_iota(I32, (chunk, quads), 1)
        return (col == (slot >> 2)) & (picks == (slot & 3))

    def enter(i, carry):
        rows = pl.ds(pl.multiple_of(i * chunk, chunk), chunk)
        hit = shown(i)
        one = jnp.where(hit, 1.0, 0.0)
        one_b = one.astype(BF)
        vis = jnp.sum(one, 1, keepdims=True)
        slot = slot_of(i, 1)
        quad = slot >> 2
        end = 0
        first = jnp.zeros((chunk, 1), I32)
        ratio = jnp.full((chunk, 1), gsd[m, 0, 0])
        for k in range(images - 1):
            end = end + sizes[m, 0, k]
            over = quad >= end
            first = jnp.where(over, end, first)
            ratio = jnp.where(over, gsd[m, 0, k + 1], ratio)
        angle = (slot - 4 * first).astype(F32) * ratio
        sine, cosine = wave_codes(angle * freq[...])
        tok = dot(one_b, emb_s[0], 1, 0) + dot(one_b, emb_s[1], 1, 0) + (1.0 - vis) * bias[7:8]
        x_s[rows, :half] = tok[:, :half] + sine
        x_s[rows, half:] = tok[:, half:] + cosine
        n, _ = norm_parts(x_s[rows, :])
        n1 = (n * gain[0:1] + bias[0:1]).astype(BF)
        n_s[rows, :] = n1
        for part in range(3):
            cols = slice(part * width, (part + 1) * width)
            got = dot(n1, wqkv[:, cols], 1, 0)
            if part == 0:
                got = (got + bias[1:2]) * (dh**-0.5 * LOG2E)
            if part == 2:
                got = got + bias[2:3]
            packed[cols, rows] = got.astype(BF).T
        move = lax.broadcasted_iota(I32, (chunk, slots), 1) == slot_of(i, slots)
        cot_s[rows, :] = dot(jnp.where(move, 1.0, 0.0).astype(BF), cot_ref[...], 1, 0).astype(BF)
        return carry

    lax.fori_loop(0, parts, enter, 0)
    sides = [slice(0, slots // 2), slice(slots // 2, slots)]

    def head(h, carry):
        for side, cols in enumerate(sides):
            attend_forward_kept(
                packed, mixed, scale, kept, qr, kr, h, side, width, dh, cols
            )
        return carry

    lax.fori_loop(0, HEADS, head, 0, unroll=2)
    for copy in loads:
        copy.wait()
    small[...] = jnp.zeros(small.shape, F32)
    tile = 512

    def middle(i, carry):
        rows = pl.ds(pl.multiple_of(i * chunk, chunk), chunk)
        res = x_s[rows, :] + dot(mixed[:, rows], wo[...], 0, 0) + bias[3:4]
        n, _ = norm_parts(res)
        n2 = (n * gain[1:2] + bias[4:5]).astype(BF)
        n2_s[rows, :] = n2
        dy = cot_s[rows, :]
        acc = jnp.zeros((chunk, width), F32)
        for t in range(hidden // tile):
            cols = slice(t * tile, (t + 1) * tile)
            u = dot(n2, w1[:, cols], 1, 0) + up_bias[:, cols].astype(F32)
            hid, dif = gelu_parts(u)
            hid_s[rows, cols] = hid.astype(BF)
            du = (dot(dy, w2[cols, :], 1, 1) * dif).astype(BF)
            du_s[rows, cols] = du
            row, col = divmod(t * tile, width)
            small[10 + row : 11 + row, col : col + tile] += jnp.sum(
                du.astype(F32), 0, keepdims=True
            )
            acc = acc + dot(du, w1[:, cols], 1, 1)
        dv, d_gain, d_shift = norm_back(res, gain[1:2], acc)
        dyf = dy.astype(F32)
        dres = dyf + dv
        res_s[rows, :] = dres
        da = dres.astype(BF)
        small[1:2, :] += d_gain
        small[5:6, :] += jnp.sum(da.astype(F32), 0, keepdims=True)
        small[6:7, :] += d_shift
        small[7:8, :] += jnp.sum(dyf, 0, keepdims=True)
        dmix[:, rows] = dot(wo[...], da, 1, 1).astype(BF)
        return carry

    lax.fori_loop(0, parts, middle, 0)

    def place(values, offset, r, wide):
        for a in range(values.shape[0] // (2 * r)):
            for cc in range(2):
                at = (a * 2 + cc) * r
                for y in range(2):
                    for j in range(wide):
                        lo = (y * wide + j) * half
                        grads[cc, a, y, offset + j * r : offset + (j + 1) * r, :] = values[
                            at : at + r, lo : lo + half
                        ]

    r_e, r_d, r_h = e_width // (2 * nzx), width // (2 * nzx), hidden // (2 * nzx)
    at_emb, at_qkv = 0, r_e
    at_out = at_qkv + 3 * r_d
    at_up = at_out + r_d
    at_down = at_up + (hidden // width) * r_d
    cot_all = cot_s[...]
    for t in range(hidden // 256):
        got = dot(hid_s[:, t * 256 : (t + 1) * 256], cot_all, 0, 0).astype(BF)
        for a in range(256 // r_h):
            blk = t * (256 // r_h) + a
            for y in range(2):
                grads[blk % 2, blk // 2, y, at_down : at_down + r_h, :] = got[
                    a * r_h : (a + 1) * r_h, y * half : (y + 1) * half
                ]
    n2_t = n2_s[...].T
    wide = hidden // width
    for t in range(hidden // half):
        got = dot(n2_t, du_s[:, t * half : (t + 1) * half], 1, 0).astype(BF)
        y, j = divmod(t, wide)
        for blk in range(2 * nzx):
            lo = at_up + j * r_d
            grads[blk % 2, blk // 2, y, lo : lo + r_d, :] = got[blk * r_d : (blk + 1) * r_d]
    place(dot(mixed[...], res_s[...].astype(BF), 1, 0).astype(BF), at_out, r_d, 1)

    def head_back(h, carry):
        attend_backward_kept(packed, mixed, scale, kept, dmix, h, width, dh, sides)
        return carry

    late = at_out if r_d % 16 == 0 else 0
    early = pl.ds(late, grads.shape[3] - late)
    outs = [
        pltpu.make_async_copy(grads.at[1 - c, :, :, early], gs_h.at[:, :, early], sems.at[0]),
        pltpu.make_async_copy(grads.at[c, :, :, early], gk_h.at[:, :, early], sems.at[1]),
    ]
    if late:
        for copy in outs:
            copy.start()
    lax.fori_loop(0, HEADS, head_back, 0, unroll=2)
    n1_t = n_s[...].T
    for t in range(3 * width // half):
        got = dot(n1_t, packed[t * half : (t + 1) * half, :], 1, 1).astype(BF)
        y, j = divmod(t, 3)
        for blk in range(2 * nzx):
            lo = at_qkv + j * r_d
            grads[blk % 2, blk // 2, y, lo : lo + r_d, :] = got[blk * r_d : (blk + 1) * r_d]
    sums = dot(jnp.ones((16, slots), BF), packed[...], 1, 1)
    small[3:4, :] = sums[0:1, :width]
    small[4:5, :] = sums[0:1, 2 * width :]
    demb_s[...] = jnp.zeros(demb_s.shape, F32)

    def leave(i, carry):
        rows = pl.ds(pl.multiple_of(i * chunk, chunk), chunk)
        e = dot(wqkv[...], packed[:, rows], 1, 0).T
        dv, d_gain, d_shift = norm_back(x_s[rows, :], gain[0:1], e)
        dx = res_s[rows, :] + dv
        hit = jnp.where(shown(i), 1.0, 0.0)
        vis = jnp.sum(hit, 1, keepdims=True)
        demb_s[...] += dot(hit.astype(BF), dx.astype(BF), 0, 0)
        small[0:1, :] += d_gain
        small[2:3, :] += d_shift
        small[9:10, :] += jnp.sum((1.0 - vis) * dx, 0, keepdims=True)
        return carry

    lax.fori_loop(0, parts, leave, 0)
    demb = demb_s[...]
    small[8:9, :] = jnp.sum(demb, 0, keepdims=True)
    demb = demb.astype(BF)
    dact = dot(demb, wemb[...], 1, 1)
    dact_ref[...] = dact.astype(BF)
    lower, upper = dact[:, : e_width // 2], dact[:, e_width // 2 :]
    dh_own[...] = jnp.where(m == 0, lower, upper).astype(BF)
    dh_other[...] = jnp.where(m == 0, upper, lower).astype(BF)
    place(dot(act_ref[...], demb, 0, 0).astype(BF), at_emb, r_e, 1)
    if late:
        first = pl.ds(0, late)
        rest = [
            pltpu.make_async_copy(grads.at[1 - c, :, :, first], gs_h.at[:, :, first], sems.at[2]),
            pltpu.make_async_copy(grads.at[c, :, :, first], gk_h.at[:, :, first], sems.at[3]),
        ]
        for copy in rest:
            copy.start()
        outs = outs + rest
    else:
        for copy in outs:
            copy.start()
    for copy in outs:
        copy.wait()


def decoder(info, sizes, gsd, picks, act, cot, gains, biases, up_bias, wemb, wqkv, wo, w1, w2, nzx):
    quads, e_width = act.shape
    slots, width = cot.shape
    hidden = w1.shape[1]
    total = e_width + 4 * width + hidden
    rows = (total + hidden // width * width) // (2 * nzx)
    freq = np.exp(np.arange(width // 2) * (-2.0 * math.log(10000.0) / width))
    freq = jnp.asarray(freq.astype(np.float32)[None, :])
    block = jax.ShapeDtypeStruct((nzx, 2, rows, width // 2), BF)
    return pl.pallas_call(
        decoder_kernel,
        out_shape=(
            jax.ShapeDtypeStruct((quads, e_width), BF),
            jax.ShapeDtypeStruct((quads, e_width // 2), BF),
            jax.ShapeDtypeStruct((quads, e_width // 2), BF),
            block,
            block,
            jax.ShapeDtypeStruct((16, width), F32),
        ),
        in_specs=[SM, SM, SM] + [VM] * 9 + [ANY] * 3,
        out_specs=(VM, VM, VM, ANY, ANY, VM),
        scratch_shapes=[
            pltpu.VMEM((slots, width), F32),
            pltpu.VMEM((slots, width), BF),
            pltpu.VMEM((3 * width, slots), BF),
            pltpu.VMEM((width, slots), BF),
            pltpu.VMEM((HEADS, slots), F32),
            pltpu.VMEM((slots, width), F32),
            pltpu.VMEM((slots, width), BF),
            pltpu.VMEM((slots, hidden), BF),
            pltpu.VMEM((slots, hidden), BF),
            pltpu.VMEM((slots, width), BF),
            pltpu.VMEM((width, slots), BF),
            pltpu.VMEM((2 * HEADS, slots // 2, slots // 2), BF),
            pltpu.VMEM((2, quads, width), BF),
            pltpu.VMEM((quads, width), F32),
            pltpu.VMEM((2, nzx, 2, rows, width // 2), BF),
            pltpu.VMEM(wo.shape, BF),
            pltpu.VMEM(w1.shape, BF),
            pltpu.VMEM(w2.shape, BF),
            pltpu.VMEM((16, slots), BF),
            pltpu.VMEM((16, slots), BF),
            pltpu.SemaphoreType.DMA((8,)),
        ],
        compiler_params=pltpu.CompilerParams(vmem_limit_bytes=VMEM_LIMIT),
        cost_estimate=TINY,
        name="decoder",
    )(info, sizes, gsd, picks, freq, act, cot, gains, biases, up_bias, wemb, wqkv, wo, w1, w2)


def pick_call(body, sel, arrays, specs, out_shape, out_specs, grid, name, deps=(), scratch=(), cost=None):
    count = len(arrays)

    def run(*refs):
        body(refs[0], *refs[1 : 1 + count], *refs[1 + count + len(deps) :])

    return pl.pallas_call(
        run,
        grid_spec=pltpu.PrefetchScalarGridSpec(
            num_scalar_prefetch=1,
            grid=grid,
            in_specs=list(specs) + [ANY] * len(deps),
            out_specs=out_specs,
            scratch_shapes=list(scratch),
        ),
        out_shape=out_shape,
        compiler_params=pltpu.CompilerParams(vmem_limit_bytes=VMEM_LIMIT),
        cost_estimate=cost or TINY,
        name=name,
    )(sel, *arrays, *deps)


def down_grad(sel, hids, dys, deps):
    nz, _, r, tokens = hids[0].shape
    half = dys[0].shape[1]
    count = len(hids)

    def body(s, *refs):
        got = dot(refs[0][...], refs[count][...], 1, 0)
        for i in range(1, count):
            got = got + dot(refs[i][...], refs[count + i][...], 1, 0)
        refs[-1][...] = got.astype(BF)

    lhs = pl.BlockSpec((None, None, r, tokens), lambda z, s: (z, s[0], 0, 0))
    rhs = pl.BlockSpec((tokens, half), lambda z, s: (0, 0))
    return pick_call(
        body, sel, tuple(hids) + tuple(dys), [lhs] * count + [rhs] * count,
        jax.ShapeDtypeStruct((nz, r, half), BF),
        pl.BlockSpec((None, r, half), lambda z, s: (z, 0, 0)),
        (nz,), "down_grad", deps, (), LONG,
    )


def down_fold(place, hids, dys, got, deps):
    nz, _, r, tokens = hids[0].shape
    half = dys[0].shape[1]
    count = len(hids)

    def body(s, *refs):
        total = dot(refs[0][...], refs[count][...], 1, 0)
        for i in range(1, count):
            total = total + dot(refs[i][...], refs[count + i][...], 1, 0)
        total = (total + refs[2 * count][...].astype(F32)).astype(BF)
        step = pl.program_id(0)

        @pl.when(step < 2)
        def first():
            refs[-2][...] = total

        @pl.when(step >= 2)
        def second():
            refs[-1][...] = total

    def block(i, s):
        base = jnp.where(i < 2, s[2] ^ 1, s[2])
        return jnp.where((i & 1) == 1, 3 - base, base)

    lhs = pl.BlockSpec((None, None, r, tokens), lambda i, s: (block(i, s), s[3] & 1, 0, 0))
    rhs = pl.BlockSpec((tokens, half), lambda i, s: (0, 0))
    more = pl.BlockSpec((None, r, half), lambda i, s: (block(i, s), 0, 0))
    shape = jax.ShapeDtypeStruct((2, r, half), BF)
    outs = (
        pl.BlockSpec((None, r, half), lambda i, s: (jnp.minimum(i, 1), 0, 0)),
        pl.BlockSpec((None, r, half), lambda i, s: (jnp.maximum(i - 2, 0), 0, 0)),
    )
    return pick_call(
        body, place, tuple(hids) + tuple(dys) + (got,), [lhs] * count + [rhs] * count + [more],
        (shape, shape), outs, (4,), "down_fold", deps,
    )


def up_grad(sel, xk, xr, duk, dur, deps):
    nzx, rows, tokens = xk.shape
    r, half = rows // 3, 512
    cols = 4

    def body(s, a, b, da, db, out):
        lhs = a[...].reshape(nzx * r, tokens)
        lhr = b[...].reshape(nzx * r, tokens)
        got = dot(lhs, da[...], 1, 0) + dot(lhr, db[...], 1, 0)
        out[...] = got.astype(BF).reshape(nzx, r, half)

    lhs = pl.BlockSpec((nzx, r, tokens), lambda j, s: (0, 2, 0))
    rhs = pl.BlockSpec((tokens, half), lambda j, s: (0, s[0] * cols + j))
    return pick_call(
        body, sel, (xk, xr, duk, dur), [lhs, lhs, rhs, rhs],
        jax.ShapeDtypeStruct((nzx, cols * r, half), BF),
        pl.BlockSpec((nzx, r, half), lambda j, s: (0, j, 0)),
        (cols,), "up_grad", deps,
    )


def up_turn(place, xk, xr, duk, dur, got, deps):
    nzx, rows, tokens = xk.shape
    nz, r, half, cols = nzx // 2, rows // 3, 512, 4

    def body(s, ag, bg, ak, bk, da, db, gg, gk, give, keep):
        for a, b, g, out in ((ag, bg, gg, give), (ak, bk, gk, keep)):
            total = dot(a[...].reshape(nz * r, tokens), da[...], 1, 0)
            total = total + dot(b[...].reshape(nz * r, tokens), db[...], 1, 0)
            total = total + g[...].reshape(nz * r, half).astype(F32)
            out[...] = total.astype(BF).reshape(nz, r, half)

    def lhs(flip):
        return pl.BlockSpec((nz, None, r, tokens), lambda j, s: (0, s[0] ^ flip, 2, 0))

    def more(flip):
        return pl.BlockSpec((nz, None, r, half), lambda j, s: (0, s[0] ^ flip, j, 0))

    rhs = pl.BlockSpec((tokens, half), lambda j, s: (0, s[1] * cols + j))
    four = (nz, 2, rows, tokens)
    a, b = xk.reshape(four), xr.reshape(four)
    got = got.reshape(nz, 2, cols * r, half)
    shape = jax.ShapeDtypeStruct((nz, cols * r, half), BF)
    out = pl.BlockSpec((nz, r, half), lambda j, s: (0, j, 0))
    return pick_call(
        body, place, (a, b, a, b, duk, dur, got, got),
        [lhs(1), lhs(1), lhs(0), lhs(0), rhs, rhs, more(1), more(0)],
        (shape, shape), (out, out),
        (cols,), "up_turn", deps,
    )


def qk_turn(place, xk, xr, dpk, dpr, got, deps):
    nzx, rows, tokens = xk.shape
    nz, r, half = nzx // 2, rows // 3, 512

    def body(s, a, b, dg, eg, dk, ek, gg, gk, give, keep):
        lhs, lhr = a[...].reshape(nz * r, tokens), b[...].reshape(nz * r, tokens)
        for d, e, g, out in ((dg, eg, gg, give), (dk, ek, gk, keep)):
            total = dot(lhs, d[...], 1, 1) + dot(lhr, e[...], 1, 1)
            total = total + g[...].reshape(nz * r, half).astype(F32)
            out[...] = total.astype(BF).reshape(nz, r, half)

    lhs = pl.BlockSpec((nz, None, r, tokens), lambda j, s: (0, s[0], 0, 0))

    def rhs(flip):
        return pl.BlockSpec((half, tokens), lambda j, s: ((s[1] ^ flip) * 2 + j, 0))

    def more(flip):
        return pl.BlockSpec((nz, None, r, half), lambda j, s: (0, s[1] ^ flip, j, 0))

    four = (nz, 2, rows, tokens)
    shape = jax.ShapeDtypeStruct((nz, 2 * r, half), BF)
    out = pl.BlockSpec((nz, r, half), lambda j, s: (0, j, 0))
    return pick_call(
        body, place, (xk.reshape(four), xr.reshape(four), dpk, dpr, dpk, dpr, got, got),
        [lhs, lhs, rhs(1), rhs(1), rhs(0), rhs(0), more(1), more(0)],
        (shape, shape), (out, out), (2,), "qk_turn", deps,
    )


def table_blocks(r):
    return -(-(TABLE // 2) // r)


def put_table(out, first, table, r):
    lines = table.shape[0]
    for k in range(table_blocks(r)):
        count = min(r, lines - k * r)
        out[first + k, :count] = table[k * r : k * r + count]
        if count < r:
            out[first + k, count:r] = jnp.zeros((r - count, table.shape[1]), BF)


def take_table(ref, first, r):
    lines = TABLE // 2
    parts = [ref[first + k, : min(r, lines - k * r)] for k in range(table_blocks(r))]
    return jnp.concatenate(parts, 0) if len(parts) > 1 else parts[0]


def vo_turn(place, xk, xr, dpk, dpr, dak, dar, got, table, deps):
    nzx, rows, tokens = xk.shape
    nz, r, half = nzx // 2, rows // 3, 512
    tail = table_blocks(r)

    def body(s, ag, bg, ak, bk, d, e, f, h, g, own, give, keep, sums):
        came = g[:nzx].reshape(nz, 2, r, half)
        lower, upper = came[:, 0].astype(F32), came[:, 1].astype(F32)
        first = s[0] == 0
        sides = (jnp.where(first, upper, lower), jnp.where(first, lower, upper))

        def run(dx, ex, cb):
            for a, b, c, out in ((ag, bg, sides[0], give), (ak, bk, sides[1], keep)):
                total = dot(a[...].reshape(nz * r, tokens), dx[...], 1, cb)
                total = total + dot(b[...].reshape(nz * r, tokens), ex[...], 1, cb)
                total = total.reshape(nz, r, half) + c
                out[:nz] = total.astype(BF)

        @pl.when(pl.program_id(0) == 0)
        def qkv():
            run(d, e, 1)
            total = own[...].astype(F32) + take_table(g, nzx, r).astype(F32)
            sums[...] = total.astype(BF)
            put_table(give, nz, total.astype(BF), r)

        @pl.when(pl.program_id(0) == 1)
        def proj():
            run(f, h, 0)
            give[nz:] = jnp.zeros((tail, r, half), BF)

    def lhs(flip):
        return pl.BlockSpec((nz, None, r, tokens), lambda i, s: (0, s[0] ^ flip, i, 0))

    rhs = pl.BlockSpec((half, tokens), lambda i, s: (s[1], 0))
    other = pl.BlockSpec((tokens, half), lambda i, s: (0, dak.shape[1] // half - 2 + s[1]))
    tab = pl.BlockSpec(table.shape, lambda i, s: (0, 0))
    four = (nz, 2, rows, tokens)
    a, b = xk.reshape(four), xr.reshape(four)
    block = lambda n: pl.BlockSpec((n, r, half), lambda i, s: (0, i, 0))
    shape = lambda n: jax.ShapeDtypeStruct((n, 2 * r, half), BF)
    return pick_call(
        body, place, (a, b, a, b, dpk, dpr, dak, dar, got, table),
        [lhs(1), lhs(1), lhs(0), lhs(0), rhs, rhs, other, other, block(nzx + tail), tab],
        (shape(nz + tail), shape(nz), jax.ShapeDtypeStruct(table.shape, BF)),
        (block(nz + tail), block(nz), tab), (2,), "vo_turn", deps,
    )


def qk_grad(sel, xk, xr, dpk, dpr, deps):
    nzx, rows, tokens = xk.shape
    nz, r, half = nzx // 2, rows // 3, 512

    def body(s, a, b, da, db, out):
        lhs = a[...].reshape(nz * r, tokens)
        lhr = b[...].reshape(nz * r, tokens)
        got = dot(lhs, da[...], 1, 1) + dot(lhr, db[...], 1, 1)
        out[...] = got.astype(BF).reshape(nz, 1, r, half)

    lhs = pl.BlockSpec((nz, 1, r, tokens), lambda y, j, s: (0, s[0], 0, 0))
    rhs = pl.BlockSpec((half, tokens), lambda y, j, s: (y * 2 + j, 0))
    split = (nz, 2, rows, tokens)
    return pick_call(
        body, sel, (xk.reshape(split), xr.reshape(split), dpk, dpr), [lhs, lhs, rhs, rhs],
        jax.ShapeDtypeStruct((nz, 2, 2 * r, half), BF),
        pl.BlockSpec((nz, 1, r, half), lambda y, j, s: (0, y, j, 0)),
        (2, 2), "qk_grad", deps,
    )


def vo_grad(sel, xk, xr, dpk, dpr, dak, dar, deps):
    nzx, rows, tokens = xk.shape
    r, half = rows // 3, 512
    top, tail = dpk.shape[0] // TABLE - 1, table_blocks(r)

    def body(s, a, b, da, db, ea, eb, ta, tb, out, table):
        lhs = a[...].reshape(nzx * r, tokens)
        lhr = b[...].reshape(nzx * r, tokens)

        @pl.when(pl.program_id(0) == 0)
        def first():
            got = dot(lhs, da[...], 1, 1) + dot(lhr, db[...], 1, 1)
            out[:nzx] = got.astype(BF).reshape(nzx, r, half)
            total = (ta[...].astype(F32) + tb[...].astype(F32)).astype(BF)
            table[:, :tokens] = total[: TABLE // 2]
            table[:, tokens:] = total[TABLE // 2 :]
            put_table(out, nzx, table[...], r)

        @pl.when(pl.program_id(0) == 1)
        def second():
            got = dot(lhs, ea[...], 1, 0) + dot(lhr, eb[...], 1, 0)
            out[:nzx] = got.astype(BF).reshape(nzx, r, half)
            out[nzx:] = jnp.zeros((tail, r, half), BF)

    lhs = pl.BlockSpec((nzx, r, tokens), lambda i, s: (0, i, 0))
    rhs = pl.BlockSpec((half, tokens), lambda i, s: (s[0], 0))
    other = pl.BlockSpec((tokens, half), lambda i, s: (0, dak.shape[1] // half - 2 + s[0]))
    behind = pl.BlockSpec((TABLE, tokens), lambda i, s: (top, 0))
    shape = (
        jax.ShapeDtypeStruct((nzx + tail, 2 * r, half), BF),
        jax.ShapeDtypeStruct((TABLE // 2, 2 * tokens), BF),
    )
    out = (
        pl.BlockSpec((nzx + tail, r, half), lambda i, s: (0, i, 0)),
        pl.BlockSpec((TABLE // 2, 2 * tokens), lambda i, s: (0, 0)),
    )
    return pick_call(
        body, sel, (xk, xr, dpk, dpr, dak, dar, dpk, dpr),
        [lhs, lhs, rhs, rhs, other, other, behind, behind], shape, out, (2,), "vo_grad", deps,
    )


def to_core(value):
    return lax.ppermute(value, "dp", [(d, d ^ 1) for d in range(lax.axis_size("dp"))])


def to_x(value):
    return lax.ppermute(value, "dp", [(d, d ^ 2) for d in range(lax.axis_size("dp"))])


def to_y(value):
    return lax.ppermute(value, "segment", [(0, 1), (1, 0)])


def to_corner(value):
    count = lax.axis_size("dp")
    pairs = [(s * count + d, (1 - s) * count + (d ^ 2)) for s in range(2) for d in range(count)]
    return lax.ppermute(value, ("segment", "dp"), pairs)


def to_z(value, step):
    count = lax.axis_size("dp")
    return lax.ppermute(value, "dp", [(d, (d + 4 * step) % count) for d in range(count)])


def to_z_pair(value):
    return lax.ppermute(value, "dp", [(d, d ^ 4) for d in range(lax.axis_size("dp"))])


def to_z_mirror(value):
    return lax.ppermute(value, "dp", [(d, d ^ 12) for d in range(lax.axis_size("dp"))])


def summed(refs):
    total = refs[0][...].astype(F32)
    for ref in refs[1:]:
        total = total + ref[...].astype(F32)
    return total


def turn(place, items, extra, deps, cost=None):
    nz = items[0][0].shape[0]
    count = 4 * len(items)

    def body(s, *refs):
        outs = refs[count + len(extra) :]
        for i in range(count // 2):
            outs[i][...] = summed(refs[2 * i : 2 * i + 2]).astype(BF)
        if extra:
            outs[-1][...] = summed(refs[count : count + 2]).astype(BF)

    def spec(shape, which, flip):
        return pl.BlockSpec((None, None) + shape[2:], lambda z, s: (z, s[which] ^ flip, 0, 0))

    arrays, specs, outs, shapes = (), [], [], []
    for kept, got, which in items:
        for flip in (1, 0):
            arrays += (kept, got)
            specs += [spec(kept.shape, which, flip)] * 2
            outs.append(pl.BlockSpec((None,) + kept.shape[2:], lambda z, s: (z, 0, 0)))
            shapes.append(jax.ShapeDtypeStruct((nz,) + kept.shape[2:], BF))
    for table in extra:
        arrays += (table,)
        specs.append(pl.BlockSpec(table.shape, lambda z, s: (0, 0)))
    if extra:
        outs.append(specs[-1])
        shapes.append(jax.ShapeDtypeStruct(extra[0].shape, BF))
    return pick_call(
        body, place, arrays, specs, tuple(shapes), tuple(outs), (nz,), "turn", deps, (), cost
    )


def fold(place, pairs, extra, deps, cost):
    nz, _, half = pairs[0][0].shape
    arrays = tuple(v for pair in pairs for v in pair) + tuple(extra)
    rows = sum(kept.shape[1] for kept, got in pairs) + (extra[0].shape[0] if extra else 0)

    def body(s, *refs):
        give, keep = refs[-2:]
        z = s[2]
        for out, first in ((give, z ^ 1), (keep, z)):
            for i, block in ((0, first), (1, 3 - first)):
                at = 0
                for p in range(len(pairs)):
                    a, b = refs[2 * p], refs[2 * p + 1]
                    r = a.shape[1]
                    out[i, at : at + r] = (a[block].astype(F32) + b[block].astype(F32)).astype(BF)
                    at += r
                if extra:
                    came = take_table(refs[2 * len(pairs) - 1], nz, refs[1].shape[1] // 2)
                    out[i, at:] = (refs[2 * len(pairs)][...].astype(F32) + came.astype(F32)).astype(BF)

    whole = lambda array: pl.BlockSpec(array.shape, lambda i, s: (0,) * array.ndim)
    shape = jax.ShapeDtypeStruct((2, rows, half), BF)
    out = pl.BlockSpec((2, rows, half), lambda i, s: (0, 0, 0))
    return pick_call(
        body, place, arrays, [whole(a) for a in arrays], (shape, shape), (out, out),
        (1,), "fold", deps, (), cost,
    )


def fold_wide(place, kept, got, deps):
    _, rows, cols = kept.shape

    def body(s, a, b, give, keep):
        total = (a[...].astype(F32) + b[...].astype(F32)).astype(BF)
        step = pl.program_id(0)

        @pl.when(step < 2)
        def first():
            give[...] = total

        @pl.when(step >= 2)
        def second():
            keep[...] = total

    def block(i, s):
        base = jnp.where(i < 2, s[2] ^ 1, s[2])
        return jnp.where((i & 1) == 1, 3 - base, base)

    spec = pl.BlockSpec((None, rows, cols), lambda i, s: (block(i, s), 0, 0))
    shape = jax.ShapeDtypeStruct((2, rows, cols), BF)
    outs = (
        pl.BlockSpec((None, rows, cols), lambda i, s: (jnp.minimum(i, 1), 0, 0)),
        pl.BlockSpec((None, rows, cols), lambda i, s: (jnp.maximum(i - 2, 0), 0, 0)),
    )
    return pick_call(
        body, place, (kept, got), [spec, spec], (shape, shape), outs, (4,), "fold_wide", deps
    )


def settle(place, parts, which, deps, cost=None):
    rows, cols = parts[0].shape[-2] // 2, parts[0].shape[-1]
    count = len(parts)

    def body(s, *refs):
        refs[-2][...] = summed(refs[:count]).astype(BF)
        refs[-1][...] = summed(refs[count : 2 * count]).astype(BF)

    def spec(array, flip):
        if array.ndim == 3:
            return pl.BlockSpec((None, rows, cols), lambda i, s: (0, s[which] ^ flip, 0))
        return pl.BlockSpec((rows, cols), lambda i, s: (s[which] ^ flip, 0))

    out = pl.BlockSpec((rows, cols), lambda i, s: (0, 0))
    shape = jax.ShapeDtypeStruct((rows, cols), BF)
    return pick_call(
        body, place, tuple(parts) * 2, [spec(p, 1) for p in parts] + [spec(p, 0) for p in parts],
        (shape, shape), (out, out), (1,), "settle", deps, (), cost,
    )


def mirror(place, kept, got, deps):
    _, rows, half = kept.shape

    def body(s, a, b, out):
        out[...] = (a[...].astype(F32) + b[...].astype(F32)).astype(BF)

    spec = pl.BlockSpec((None, rows, half), lambda i, s: (1, 0, 0))
    return pick_call(
        body, place, (kept, got), [spec, spec], jax.ShapeDtypeStruct((rows, half), BF),
        pl.BlockSpec((rows, half), lambda i, s: (0, 0)), (1,), "mirror", deps,
    )


def spread(place, pairs, extra, deps):
    nz, _, half = pairs[0][0].shape
    arrays = tuple(v for pair in pairs for v in pair) + tuple(extra)
    rows = sum(kept.shape[1] for kept, got in pairs) + (extra[0].shape[0] if extra else 0)

    def body(s, *refs):
        for step in range(nz):
            block = lax.rem(s[2] + step, nz)
            out = refs[len(arrays) + step]
            at = 0
            for p in range(len(pairs)):
                a, b = refs[2 * p], refs[2 * p + 1]
                r = a.shape[1]
                total = a[block].astype(F32) + b[block].astype(F32)
                out[at : at + r] = total.astype(out.dtype)
                at += r
            if extra:
                came = take_table(refs[2 * len(pairs) - 1], nz, refs[1].shape[1] // 2)
                total = refs[2 * len(pairs)][...].astype(F32) + came.astype(F32)
                out[at:] = total.astype(out.dtype)

    whole = lambda array: pl.BlockSpec(array.shape, lambda i, s: (0,) * array.ndim)
    shapes = [jax.ShapeDtypeStruct((rows, half), F32)]
    shapes += [jax.ShapeDtypeStruct((rows, half), BF)] * (nz - 1)
    out = pl.BlockSpec((rows, half), lambda i, s: (0, 0))
    return pick_call(
        body, place, arrays, [whole(a) for a in arrays], tuple(shapes), (out,) * nz,
        (1,), "spread", deps,
    )


def finish(place, parts, cuts, vectors, deps, cost=None):
    half = parts[0].shape[-1]
    count = len(parts)
    taken = sum(rows * wide for rows, wide in cuts)
    table = parts[0].shape[-2] - taken

    def body(s, *refs):
        outs = refs[count:]
        at = 0
        for (rows, wide), out in zip(cuts, outs):
            for j in range(wide):
                lo = at + j * rows
                total = refs[0][lo : lo + rows].astype(F32)
                for ref in refs[1:count]:
                    total = total + ref[lo : lo + rows].astype(F32)
                out[:, j * half : (j + 1) * half] = total
            at += rows * wide
        if vectors:
            sums = refs[-1]
            total = refs[0][at:].astype(F32)
            for ref in refs[1:count]:
                total = total + ref[at:].astype(F32)
            sums[...] = total
            for (rows, where, length), out in zip(vectors, outs[len(cuts) :]):
                for k in range(rows):
                    row, col = where(s, k)
                    line = sums[pl.ds(row, 1), :]
                    line = pltpu.roll(line, lax.rem(half - col, half), 1)
                    out[k : k + 1, :] = line[:, :length]

    whole = lambda shape: pl.BlockSpec(shape, lambda i, s: (0, 0))
    first = lambda shape: (
        whole(shape) if len(shape) == 2 else pl.BlockSpec((None,) + shape[1:], lambda i, s: (0, 0, 0))
    )
    shapes = [(rows, wide * half) for rows, wide in cuts]
    shapes += [(rows, length) for rows, where, length in vectors]
    scratch = [pltpu.VMEM((table, half), F32)] if vectors else []
    return pick_call(
        body, place, tuple(parts), [first(p.shape) for p in parts],
        tuple(jax.ShapeDtypeStruct(shape, F32) for shape in shapes),
        tuple(whole(shape) for shape in shapes), (1,), "finish", deps, scratch, cost,
    )


def along_z(place, pairs, extra, deps, cost=None):
    if pairs[0][0].shape[0] == 4:
        give, keep = fold(place, pairs, extra, deps, cost)
        return (keep, to_z_pair(give))
    blocks = spread(place, pairs, extra, deps)
    return (blocks[0],) + tuple(to_z(b, step + 1) for step, b in enumerate(blocks[1:]))


def across_z(state):
    if state[0].ndim == 3:
        give = (state[0][1].astype(F32) + state[1][1].astype(F32)).astype(BF)
        return state + (to_z_mirror(give),), give
    return state, state[0]


def local(
    patches, cotangent, image_quads, keep_pick, image_gsd,
    enc_gains, enc_biases, enc_qkv, enc_proj, enc_fc1, enc_fc1_bias, enc_fc2,
    dec_embed, dec_gains, dec_biases, dec_qkv, dec_proj, dec_fc1, dec_fc1_bias, dec_fc2,
):
    d = lax.axis_index("dp")
    y = lax.axis_index("segment")
    count = lax.axis_size("dp")
    c, x, z = d & 1, (d >> 1) & 1, d >> 2
    nzx = count // 2
    nz = nzx // 2
    info = jnp.stack([y, c, x]).astype(I32)
    place = jnp.stack([x, y, z, d]).astype(I32)
    other_x, other_y = (1 - x).reshape(1), (1 - y).reshape(1)
    own_c, other_c = c.reshape(1), (1 - c).reshape(1)
    row_x = patches[0]
    row_cot = cotangent[0]
    d_enc, d_dec = enc_gains.shape[1], dec_gains.shape[1]
    f_enc, f_dec = enc_fc1.shape[1], dec_fc1.shape[1]
    r_h, r_d = f_enc // count, d_enc // count
    s_d, s_h = d_dec // count, f_dec // count
    split = lambda v: v.reshape((nz, 2) + v.shape[1:])

    act, xs, xk, hs, hk, packed, lse, mixed, resid, slope = enc_forward(
        info, image_quads, row_x, enc_gains, enc_biases, enc_fc1_bias[None, :],
        enc_qkv, enc_proj, enc_fc1, enc_fc2, nzx,
    )
    xr = to_core(xs)
    hids = (hk, to_x(hs), to_y(hk), to_corner(hs))
    dact, dh_own, dh_other, dec_give, dec_keep, dec_small = decoder(
        info, image_quads, image_gsd, keep_pick, act, row_cot, dec_gains, dec_biases,
        dec_fc1_bias[None, :], dec_embed, dec_qkv, dec_proj, dec_fc1, dec_fc2, nzx,
    )
    dec_got = to_core(dec_give)
    dys = (dh_own, to_x(dh_own), to_y(dh_other), to_corner(dh_other))
    du, dres, small_a = enc_ffn_back(
        dact, resid, slope, enc_gains, enc_fc1, enc_fc2, (xr,) + hids[1:]
    )
    dur = to_core(du)
    if nz == 4:
        block = (nz, 4 * dec_keep.shape[2], dec_keep.shape[3])
        d_give, d_keep = fold_wide(place, dec_keep.reshape(block), dec_got.reshape(block), (du,))
        d_got = to_z_pair(d_give)
    else:
        block = (nz, 2, 2 * dec_keep.shape[2], dec_keep.shape[3])
        d_give, d_keep = turn(
            place, ((dec_keep.reshape(block), dec_got.reshape(block), 0),), (), (du,)
        )
        d_got = to_x(d_give)
    w_give = down_grad(other_c, hids, dys, (d_keep,))
    w_got = to_core(w_give)
    f_give = up_grad(other_y, xk, xr, du, dur, (w_give,))
    f_got = to_y(f_give)
    if nz == 4:
        w_give, w_keep = down_fold(place, hids, dys, w_got, (f_give,))
        w_z = (w_keep, to_z_pair(w_give))
    else:
        w_keep = down_grad(own_c, hids, dys, (f_give,))
        w_z = along_z(place, ((w_keep, w_got),), (), ())
    dx, dp, dp_one = enc_att_back(
        info, image_quads, row_x, du, dres, packed, lse, mixed, enc_gains, small_a, dec_small,
        enc_qkv, enc_proj, (w_z[0],),
    )
    dp_oner = to_core(dp_one)
    dpr = to_core(dp)
    if nz == 4:
        dec_z, last_d = across_z((d_keep, d_got))
    else:
        halves = (nz, 2, d_keep.shape[1] // 2, d_keep.shape[2])
        d_give, d_keep = turn(
            place, ((d_keep.reshape(halves), d_got.reshape(halves), 1),), (), (dx,)
        )
        last_d = d_keep
        dec_z = along_z(place, ((d_keep, to_y(d_give)),), (), ())
    ta_give = qk_grad(other_x, xk, xr, dp, dpr, (dx, last_d))
    ta_got = to_x(ta_give)
    tb_give, table = vo_grad(other_y, xk, xr, dp_one, dp_oner, du, dur, (ta_give,))
    tb_got = to_y(tb_give)
    f_give, f_keep = up_turn(place, xk, xr, du, dur, f_got, (table,))
    f_got = to_x(f_give)
    ta_give, ta_keep = qk_turn(place, xk, xr, dp, dpr, ta_got, (f_keep,))
    ta_got = to_y(ta_give)
    last = ta_keep
    tb_give, tb_keep, table = vo_turn(
        place, xk, xr, dp_one, dp_oner, du, dur, tb_got, table, (last,)
    )
    tb_got = to_x(tb_give)
    last = tb_keep
    if nz == 4:
        d_give, d_keep = settle(place, dec_z, 0, (last,), REST)
        d_got = to_x(d_give)
        last = d_keep
    f_z = along_z(place, ((f_keep, f_got),), (), (last,), MORE)
    last = f_z[0]
    if nz == 4:
        give = mirror(place, w_z[0], w_z[1], (last,))
        w_z = w_z + (to_z_mirror(give),)
        last = give
    att_z = along_z(place, ((ta_keep, ta_got), (tb_keep, tb_got)), (table,), (last,))
    last = att_z[0]
    if nz == 4:
        d_give, d_keep = settle(place, (d_keep, d_got), 1, (last,))
        dec_z = (d_keep, to_y(d_give))
        last = d_keep
    (g_fc2,) = finish(place, w_z, ((r_h, 1),), (), (last,))
    last = g_fc2
    f_z, last_f = across_z(f_z)
    if len(att_z) == 2:
        give = mirror(place, att_z[0], att_z[1], (last_f, last))
        att_z = att_z + (to_z_mirror(give),)
        last = give
    h_emb, h_qkv, h_proj, h_fc1, h_fc2 = finish(
        place, dec_z, ((r_d, 1), (s_d, 3), (s_d, 1), (s_d, s_h // s_d), (s_h, 1)), (),
        (last,),
    )
    (g_fc1,) = finish(place, f_z, ((r_d, r_h // r_d),), (), (h_fc2,), SOME)

    piece, lanes = row_x.shape[0], TABLE // 2

    def spot(base, row, col):
        line = base + (col // piece) * 16 + row
        return lax.rem(line, lanes), (line // lanes) * piece + lax.rem(col, piece)

    def window(base, first, per_y, length):
        return lambda s, k: spot(base, first + s[1] * per_y + k, s[3] * length)

    def window_flat(base, first, wide, length):
        def where(s, k):
            col = (s[1] * count + s[3]) * length
            return spot(base, first + col // wide, lax.rem(col, wide))

        return where

    base = d_enc // piece * 16
    v_h, u_h = f_enc // (2 * count), f_dec // (2 * count)
    vectors = (
        (1, window(0, 0, 1, r_d), r_d),
        (3, window(0, 2, 3, r_d), r_d),
        (1, window_flat(0, 8, d_enc, v_h), v_h),
        (1, window(base, 0, 1, s_d), s_d),
        (4, window(base, 2, 4, s_d), s_d),
        (1, window_flat(base, 10, d_dec, u_h), u_h),
    )
    g_qkv, g_proj, e_gains, e_biases, e_up, d_gains, d_biases, d_up = finish(
        place, att_z, ((r_d, 3), (r_d, 1)), vectors, ()
    )
    return (
        dx[None], e_gains, e_biases, g_qkv, g_proj, g_fc1, e_up.reshape(-1), g_fc2,
        h_emb, d_gains, d_biases, h_qkv, h_proj, h_fc1, d_up.reshape(-1), h_fc2,
    )


def solution(mesh):
    rows3 = P("segment", "dp", None)
    placed = (rows3, rows3, P(None, "dp", None), P(None, "dp"), P(None, "dp", None)) + (P(),) * 15
    both, wide, flat = P("segment", "dp"), P("dp", "segment"), P(("segment", "dp"))
    return jax.shard_map(
        local,
        mesh=mesh,
        in_specs=placed,
        out_specs=(
            rows3, both, both, wide, wide, wide, flat, wide,
            wide, both, both, wide, wide, wide, flat, wide,
        ),
        check_vma=False,
    )
```
